128 devices in a mesh: row: 16 (over y, x), col: 8 (over z, core).
Axes of the slice: x: 4, y: 4, z: 4, core: 2. Of those that a mesh axis runs over, the one named last changes fastest.
Arguments:
- emission: float32 [16, 1048576], P(None, ('row', 'col')), may hold values from -6 to 6
- basis_source: bfloat16 [64, 1048576], P(None, ('row', 'col')), may hold values from -0.5 to 0.5
- basis_target: bfloat16 [64, 1048576], P(None, ('row', 'col')), may hold values from -0.75 to 0.75
- local_transfer: bfloat16 [16128, 64, 64], P(('row', 'col')), may hold values from -0.5 to 0.5
- local_sibling: bfloat16 [7936, 64, 64], P(('row', 'col')), as said below
- upper_transfer: bfloat16 [254, 64, 64], replicated, may hold values from -0.5 to 0.5
- upper_sibling: bfloat16 [254, 64, 64], replicated, as said below
- leaf_source: int32 [8192, 4], P(('row', 'col')), may hold values from 0 to 8191, as said below
- leaf_coupling: bfloat16 [8192, 4, 64, 64], P(('row', 'col')), may hold values from -0.375 to 0.375
- near_block: bfloat16 [24576, 128, 128], P(('row', 'col')), may hold values from -0.5 to 0.5
- near_target: int32 [24576], P(('row', 'col')), may hold values from 0 to 8191, as said below
- near_source: int32 [24576], P(('row', 'col')), may hold values from 0 to 8191, as said below
- near_count: int32 [128], P(('row', 'col')), may hold values from 66 to 192, as said below
Outputs:
- irradiance: float32 [16, 1048576], P(None, ('row', 'col'))
The draws below stay inside these ranges and needn't reach their ends.
Inputs may be any that keep to these rules, and one draw needn't show every extreme that they name: leaf_source[t, j] lies in the row subtree of t (the same block of 512 leaves) and differs from t by 2 or more. `near_target`: the slots of device d name target leaves of device d only; the first 64 slots of each device hold every leaf of the device once, as its own source. `near_source`: each slot's source leaf lies within one leaf of its target leaf. `near_count`: some device uses all of its slots. `local_sibling`: coupling matrices of clusters higher in the tree are larger in magnitude. `upper_sibling`: coupling matrices of clusters higher in the tree are larger in magnitude.
All inputs are finite; a program needn't handle non-finite values.
Results may differ from the reference program's by a relative error of at most 0.0005.
Values sent between devices are 32-bit elements; how exact they have to be, the bound alone decides.
A program may use at most 128 MiB of HBM per device.

```python
import math
import jax
import jax.numpy as jnp
from jax import lax

LEAF = 128
RANK = 64
RHS = 16
PARTNERS = 4
LEAF_DEV = 64
LEAVES = 8192
PATCHES = 1048576
GROUP_LEAVES = 512
LOCAL = 126
SIBS = 62
UPPER = 254
NEAR_CAP = 192
DEVICES = 128


def level_scaled(key, height):
    values = jax.random.normal(key, (height.shape[0], RANK, RANK), jnp.float32)
    values = jnp.clip(values, -4.0, 4.0)
    factor = jnp.exp2(height.astype(jnp.float32) * 0.5) / math.sqrt(RANK)
    return (values * factor[:, None, None]).astype(jnp.bfloat16)


def draw_local_sibling(key, part):
    key = jax.random.fold_in(key, 11)
    row_count = DEVICES * SIBS
    within = jnp.arange(row_count, dtype=jnp.int32) % SIBS
    height = jnp.ones((row_count,), jnp.int32)
    for section_index in range(2, 16):
        if LEAF_DEV >> section_index >= 2:
            offset = LEAF_DEV - 2 * (LEAF_DEV >> section_index)
            height = height + (within >= offset).astype(jnp.int32)
    return level_scaled(key, height)


def draw_upper_sibling(key, part):
    key = jax.random.fold_in(key, 13)
    within = jnp.arange(UPPER, dtype=jnp.int32)
    height = jnp.full((UPPER,), LEAF_DEV.bit_length() - 1, jnp.int32)
    for section_index in range(1, 16):
        if DEVICES >> section_index >= 2:
            offset = 2 * DEVICES - 2 * (DEVICES >> section_index)
            height = height + (within >= offset).astype(jnp.int32)
    return level_scaled(key, height)


def draw_leaf_source(key, part):
    key = jax.random.fold_in(key, 7)
    target_leaf = jnp.arange(LEAVES, dtype=jnp.int32)[:, None]
    offset = jax.random.randint(key, (LEAVES, PARTNERS), 2, GROUP_LEAVES - 1, dtype=jnp.int32)
    base_leaf = target_leaf // GROUP_LEAVES * GROUP_LEAVES
    return base_leaf + (target_leaf % GROUP_LEAVES + offset) % GROUP_LEAVES


def near_pairs(key):
    device = jnp.arange(DEVICES, dtype=jnp.int32)[:, None]
    local_leaf = jnp.arange(LEAF_DEV, dtype=jnp.int32)[None, :]
    own_leaf = device * LEAF_DEV + local_leaf
    device_keys = jax.random.split(jax.random.fold_in(key, 5), DEVICES)
    middle = jax.vmap(lambda single: jax.random.permutation(single, 2 * LEAF_DEV - 2))(device_keys).astype(jnp.int32) + 1
    edges = jnp.broadcast_to(jnp.array([0, 2 * LEAF_DEV - 1], jnp.int32)[None, :], (DEVICES, 2))
    ordering = jnp.concatenate([edges, middle], axis=1)
    direction = 2 * (ordering % 2) - 1
    other_target = device * LEAF_DEV + ordering // 2
    other_source = jnp.clip(other_target + direction, 0, LEAVES - 1)
    target_all = jnp.concatenate([own_leaf, other_target], axis=1).reshape(-1)
    source_all = jnp.concatenate([own_leaf, other_source], axis=1).reshape(-1)
    return (target_all, source_all)


def draw_near_target(key, part):
    return near_pairs(key)[0]


def draw_near_source(key, part):
    return near_pairs(key)[1]


def draw_near_count(key, part):
    key = jax.random.fold_in(key, 17)
    first_key, second_key, third_key = jax.random.split(key, 3)
    first_draw = jax.random.randint(first_key, (DEVICES,), 0, 2 * LEAF_DEV - 1, dtype=jnp.int32)
    second_draw = jax.random.randint(second_key, (DEVICES,), 0, 2 * LEAF_DEV - 1, dtype=jnp.int32)
    fullest = jax.random.randint(third_key, (), 0, DEVICES, dtype=jnp.int32)
    counted = LEAF_DEV + 2 + jnp.minimum(first_draw, second_draw)
    return jnp.where(jnp.arange(DEVICES, dtype=jnp.int32) == fullest, 3 * LEAF_DEV, counted).astype(jnp.int32)


def block_scale(key, dims, pieces, least, high):
    factor_of, own = 1.0, jax.random.fold_in(key, 6)
    for position, blocks in pieces:
        draws = jnp.exp(jax.random.uniform(jax.random.fold_in(own, position), (blocks,), jnp.float32, least / len(pieces), high / len(pieces)))
        factor_of = factor_of * jnp.repeat(draws, dims[position] // blocks).reshape([-1 if axis == position else 1 for axis in range(len(dims))])
    return factor_of


def normal_values(stream_key, extent, scale, most, cuts=(), kind=jnp.bfloat16):
    factor_of = block_scale(stream_key, extent, cuts, -0.22, 0.18) if cuts else 1.0
    values = jax.random.normal(stream_key, extent, jnp.float32) * scale * factor_of
    return jnp.minimum(jnp.maximum(values, -most), most).astype(kind)


def setup_inputs(seed: int = 0) -> dict:
    streams_of = jax.random.split(jax.random.key(seed), 14)
    emission = normal_values(streams_of[0], (RHS, PATCHES), 1.0, 6.0, ((1, 128),), jnp.float32)
    basis_source = normal_values(streams_of[1], (RANK, PATCHES), LEAF ** -0.5, 0.5, ((1, 128),))
    basis_target = normal_values(streams_of[2], (RANK, PATCHES), RANK ** -0.5, 0.75, ((1, 128),))
    local_transfer = normal_values(streams_of[3], (DEVICES * LOCAL, RANK, RANK), (2 * RANK) ** -0.5, 0.5, ((0, 128),))
    local_sibling = draw_local_sibling(jax.random.fold_in(streams_of[13], 71), 0)
    upper_transfer = normal_values(streams_of[5], (UPPER, RANK, RANK), (2 * RANK) ** -0.5, 0.5)
    upper_sibling = draw_upper_sibling(jax.random.fold_in(streams_of[13], 71), 0)
    leaf_source = draw_leaf_source(jax.random.fold_in(streams_of[13], 71), 0)
    leaf_coupling = normal_values(streams_of[8], (LEAVES, PARTNERS, RANK, RANK), (RANK * PARTNERS) ** -0.5, 0.375, ((0, 128),))
    near_block = normal_values(streams_of[9], (DEVICES * NEAR_CAP, LEAF, LEAF), LEAF ** -0.5, 0.5, ((0, 128),))
    near_target = draw_near_target(jax.random.fold_in(streams_of[13], 71), 0)
    near_source = draw_near_source(jax.random.fold_in(streams_of[13], 71), 0)
    near_count = draw_near_count(jax.random.fold_in(streams_of[13], 71), 0)
    return dict(emission=emission, basis_source=basis_source, basis_target=basis_target, local_transfer=local_transfer, local_sibling=local_sibling, upper_transfer=upper_transfer, upper_sibling=upper_sibling, leaf_source=leaf_source, leaf_coupling=leaf_coupling, near_block=near_block, near_target=near_target, near_source=near_source, near_count=near_count)


highest = lax.Precision.HIGHEST


def upward(transfer, coefficients):
    lifted = jnp.einsum('cba,cbr->car', transfer.astype(jnp.float32), coefficients, precision=highest)
    paired = lifted.reshape(lifted.shape[0] // 2, 2, RANK, RHS)
    return paired[:, 0] + paired[:, 1]


def downward(transfer, parents):
    spread = jnp.repeat(parents, 2, axis=0)
    return jnp.einsum('cab,cbr->car', transfer.astype(jnp.float32), spread, precision=highest)


def swapped(coefficients):
    cluster_count = coefficients.shape[0]
    return coefficients.reshape(cluster_count // 2, 2, RANK, RHS)[:, ::-1].reshape(cluster_count, RANK, RHS)


def couple(coupling, coefficients):
    return jnp.einsum('cab,cbr->car', coupling.astype(jnp.float32), coefficients, precision=highest)


def reference(emission, basis_source, basis_target, local_transfer, local_sibling, upper_transfer, upper_sibling, leaf_source, leaf_coupling, near_block, near_target, near_source, near_count):
    height_local = LEAF_DEV.bit_length() - 1
    height_upper = DEVICES.bit_length() - 1
    per_leaf = emission.reshape(RHS, LEAVES, LEAF)
    leaf_coef = jnp.einsum('kli,rli->lkr', basis_source.reshape(RANK, LEAVES, LEAF).astype(jnp.float32), per_leaf, precision=highest)
    local_t = local_transfer.reshape(DEVICES, 2 * LEAF_DEV - 2, RANK, RANK)
    local_s = local_sibling.reshape(DEVICES, LEAF_DEV - 2, RANK, RANK)
    transfers = []
    siblings = []
    for height in range(height_local):
        cluster_count = LEAF_DEV >> height
        offset = 2 * LEAF_DEV - 2 * cluster_count
        transfers.append(local_t[:, offset:offset + cluster_count].reshape(DEVICES * cluster_count, RANK, RANK))
        if height >= 1:
            first = LEAF_DEV - 2 * cluster_count
            siblings.append(local_s[:, first:first + cluster_count].reshape(DEVICES * cluster_count, RANK, RANK))
        else:
            siblings.append(None)
    for section_index in range(height_upper):
        cluster_count = DEVICES >> section_index
        offset = 2 * DEVICES - 2 * cluster_count
        transfers.append(upper_transfer[offset:offset + cluster_count])
        siblings.append(upper_sibling[offset:offset + cluster_count])
    levels = [leaf_coef]
    for matrix in transfers:
        levels.append(upward(matrix, levels[-1]))
    far_coef = jnp.zeros((1, RANK, RHS), jnp.float32)
    for height in range(len(transfers) - 1, -1, -1):
        carried = downward(transfers[height], far_coef)
        if height >= 1:
            far_coef = couple(siblings[height], swapped(levels[height])) + carried
        else:
            listed = jnp.einsum('tjab,tjbr->tar', leaf_coupling.astype(jnp.float32), leaf_coef[leaf_source], precision=highest)
            far_coef = listed + carried
    far_field = jnp.einsum('kli,lkr->rli', basis_target.reshape(RANK, LEAVES, LEAF).astype(jnp.float32), far_coef, precision=highest)
    slot_index = jnp.arange(NEAR_CAP, dtype=jnp.int32)
    blocks = near_block.reshape(DEVICES, NEAR_CAP, LEAF, LEAF)
    targets = near_target.reshape(DEVICES, NEAR_CAP)
    sources = near_source.reshape(DEVICES, NEAR_CAP)

    def visit(accumulated, item):
        block_set, target_set, source_set, live_count = item
        live_slot = (slot_index < live_count).astype(jnp.float32)
        picked = per_leaf[:, source_set]
        product = jnp.einsum('gij,rgj->rgi', block_set.astype(jnp.float32), picked, precision=highest)
        product = product * live_slot[None, :, None]
        return accumulated.at[:, target_set].add(product), None

    near_field, unused = lax.scan(visit, jnp.zeros((RHS, LEAVES, LEAF), jnp.float32), (blocks, targets, sources, near_count))
    return (far_field + near_field).reshape(RHS, PATCHES)
```

```python
import functools

import jax
import jax.numpy as jnp
from jax import lax
from jax.experimental import pallas as pl
from jax.experimental.pallas import tpu as pltpu
from jax.sharding import PartitionSpec as P

MESH = pl.DeviceIdType.MESH
F32 = jnp.float32
BF16 = jnp.bfloat16

RHS = 16
RANK = 64
LEAF = 128
LEAVES = 64
PAIRS = LEAVES // 2
PARTNERS = 4
SLOTS = 192
ROWS, COLS = 16, 8
CHUNKS = 4
PART = PAIRS // CHUNKS
HEIGHT = 6
NEAR_PARTS = 4


def dot_nn(a, b):
    return lax.dot_general(a, b, (((1,), (0,)), ((), ())), preferred_element_type=F32)


def dot_nt(a, b):
    return lax.dot_general(a, b, (((1,), (1,)), ((), ())), preferred_element_type=F32)


def split(x):
    high = x.astype(BF16)
    low = (x - high.astype(F32)).astype(BF16)
    return jnp.concatenate([high, low], axis=0)


def joined(o):
    half = o.shape[0] // 2
    return o[:half] + o[half:]


def level_offset(h):
    return 2 * LEAVES - 2 * (LEAVES >> h)


def lev_base(h):
    return PAIRS - (PAIRS >> (h - 1)) if h >= 1 else 0


def kernel(
    em_h, bs_h, bt_h, lt_h, ls_h, ut_h, us_h, lsrc, lc_h, nb_h, nt_v, nsrc, ncnt,
    out_h,
    em, bs, bt, lt, ls, ut, us, lc, nb,
    eh, halo, gath, dup, mp, mb, mu, eu, su, lev, sib, ylev, carried,
    xr, zr, upair, prod, nacc, cp, out,
    load_sem, nb_sem, bs_sem, out_sem, halo_s, halo_r,
    own_s, fwd_s, gath_r, xr_s, xr_r, zr_s, zr_r,
):
    row, col = lax.axis_index("row"), lax.axis_index("col")
    device = row * COLS + col
    z, core = col // 2, col % 2
    sibling = z * 2 + 1 - core
    znext = lax.rem(z + 1, 4)
    zprev = lax.rem(z + 3, 4)
    zfar = lax.rem(z + 2, 4)
    up_col, down_col, far_col = znext * 2 + core, zprev * 2 + core, zfar * 2 + core

    def load(src, dst, i):
        c = pltpu.make_async_copy(src, dst, load_sem.at[i])
        c.start()
        return c

    em_c = load(em_h, em, 0)
    width = 8192 // CHUNKS
    bs_c = []
    for k in range(CHUNKS):
        c = pltpu.make_async_copy(
            bs_h.at[:, pl.ds(k * width, width)], bs.at[:, pl.ds(k * width, width)], bs_sem.at[k]
        )
        c.start()
        bs_c.append(c)
    lt_c = load(lt_h, lt, 1)

    barrier = pltpu.get_barrier_semaphore()
    nxt, prv = lax.rem(device + 1, ROWS * COLS), lax.rem(device + ROWS * COLS - 1, ROWS * COLS)
    next_id = (nxt // COLS, lax.rem(nxt, COLS))
    prev_id = (prv // COLS, lax.rem(prv, COLS))
    for i in range(1, COLS):
        pl.semaphore_signal(barrier, 1, device_id=(row, lax.rem(col + i, COLS)), device_id_type=MESH)
    for i in range(1, ROWS):
        pl.semaphore_signal(barrier, 1, device_id=(lax.rem(row + i, ROWS), col), device_id_type=MESH)
    pl.semaphore_signal(barrier, 1, device_id=next_id, device_id_type=MESH)
    pl.semaphore_signal(barrier, 1, device_id=prev_id, device_id_type=MESH)

    ut_c = load(ut_h, ut, 2)
    us_c = load(us_h, us, 3)
    ls_c = load(ls_h, ls, 4)
    nb_c = []
    per = SLOTS // NEAR_PARTS
    for k in range(NEAR_PARTS):
        c = pltpu.make_async_copy(
            nb_h.at[pl.ds(k * per, per)], nb.at[pl.ds(k * per, per)], nb_sem.at[k]
        )
        c.start()
        nb_c.append(c)
    lc_c = load(lc_h, lc, 5)
    bt_c = load(bt_h, bt, 6)

    lane = lax.broadcasted_iota(jnp.int32, (RHS, 128), 1)
    first_half = lane < 64
    lane2 = lax.broadcasted_iota(jnp.int32, (2 * RHS, 128), 1)
    first_half2 = lane2 < 64

    em_c.wait()

    def split_leaf(g, carry):
        for u in range(8):
            l = g * 8 + u
            eh[l + 1] = split(em[:, pl.ds(pl.multiple_of(l * LEAF, LEAF), LEAF)])
        return carry

    lax.fori_loop(0, LEAVES // 8, split_leaf, 0)

    pl.semaphore_wait(barrier, COLS - 1 + ROWS - 1 + 2)

    halo_next = pltpu.make_async_remote_copy(
        em.at[:, pl.ds((LEAVES - 1) * LEAF, LEAF)], halo.at[0], halo_s.at[0], halo_r.at[0],
        device_id=next_id, device_id_type=MESH)
    halo_prev = pltpu.make_async_remote_copy(
        em.at[:, pl.ds(0, LEAF)], halo.at[1], halo_s.at[1], halo_r.at[1],
        device_id=prev_id, device_id_type=MESH)
    halo_next.start()
    halo_prev.start()

    def piece(owner, k):
        return gath.at[owner, pl.ds(k * PART, PART)]

    def send(owner, k, to_col, send_sem, kind):
        return pltpu.make_async_remote_copy(
            piece(owner, k), piece(owner, k), send_sem, gath_r.at[kind, k],
            device_id=(row, to_col), device_id_type=MESH)

    sends = []

    def leaf_pair(p):
        a = eh[pl.ds(2 * p + 1, 2)].reshape(64, 128)
        start = pl.multiple_of(p * 256, 256)
        w = bs[:, pl.ds(start, 256)]
        b = jnp.concatenate([w[:, :128], w[:, 128:]], axis=0)
        o = dot_nt(a, b)
        gath[col, p] = jnp.where(first_half, o[0:16] + o[16:32], o[32:48] + o[48:64])

    for k in range(CHUNKS):
        bs_c[k].wait()

        def leaf_step(g, carry, k=k):
            for u in range(4):
                leaf_pair(k * PART + g * 4 + u)
            return carry

        lax.fori_loop(0, PART // 4, leaf_step, 0)
        for n, (to_col, kind) in enumerate(((up_col, 1), (down_col, 2), (sibling, 0))):
            c = send(col, k, to_col, own_s.at[n, k], kind)
            c.start()
            sends.append(c)

    lt_c.wait()
    eye = (
        lax.broadcasted_iota(jnp.int32, (128, 126), 0)
        == lax.broadcasted_iota(jnp.int32, (128, 126), 1)
    ).astype(BF16)

    def turn_local(q, carry):
        w = jnp.concatenate([lt[q], lt[q + 32]], axis=0)
        mp[pl.ds(q, 128, stride=32), :] = dot_nt(eye, w)
        return carry

    lax.fori_loop(0, 32, turn_local, 0, unroll=2)

    def unpack(source, target, n):
        m = source[pl.ds(pl.multiple_of(n * 32, 32), 32), :].astype(BF16)
        target[n] = jnp.concatenate([m[:, :64], m[:, 64:]], axis=0)

    def unpack_local(g, carry):
        for u in range(6):
            unpack(mp, mb, g * 6 + u)
        return carry

    lax.fori_loop(0, 21, unpack_local, 0)

    def lift(pair, weights):
        return joined(dot_nn(split(pair), weights.reshape(128, 64)))

    def level_pair(h, p):
        return gath[col, p] if h == 0 else lev[lev_base(h) + p]

    for h in range(HEIGHT - 1):
        count = PAIRS >> h
        off = level_offset(h)

        def up_two(q, h=h, off=off):
            one = lift(level_pair(h, 2 * q), mb[pl.ds(off + 4 * q, 2)])
            two = lift(level_pair(h, 2 * q + 1), mb[pl.ds(off + 4 * q + 2, 2)])
            lev[lev_base(h + 1) + q] = jnp.concatenate([one, two], axis=1)

        half = count // 2
        group = min(half, 4)

        def up_step(g, carry, up_two=up_two, group=group):
            for u in range(group):
                up_two(g * group + u)
            return carry

        lax.fori_loop(0, half // group, up_step, 0)
    root = lift(lev[lev_base(5)], mb[pl.ds(level_offset(5), 2)])

    def placed(value, parity):
        return jnp.where(
            (lane >= 64).astype(jnp.int32) == parity, jnp.concatenate([value, value], axis=1), 0.0
        )

    xr[col] = placed(root, core)
    xr_copies = []
    for i in range(1, COLS):
        c = pltpu.make_async_remote_copy(
            xr.at[col], xr.at[col], xr_s.at[i], xr_r.at[i],
            device_id=(row, lax.rem(col + i, COLS)), device_id_type=MESH)
        c.start()
        xr_copies.append(c)

    def recv(owner, k, kind):
        pltpu.make_async_remote_copy(
            piece(owner, k), piece(owner, k), own_s.at[0, k], gath_r.at[kind, k],
            device_id=(row, col), device_id_type=MESH).wait_recv()

    def relay_near(k):
        recv(down_col, k, 1)
        if k < CHUNKS // 2:
            c = send(down_col, k, up_col, fwd_s.at[0, k], 3)
            c.start()
            sends.append(c)
        c = send(down_col, k, sibling, fwd_s.at[1, k], 4)
        c.start()
        sends.append(c)
        recv(up_col, k, 2)
        if k >= CHUNKS // 2:
            c = send(up_col, k, down_col, fwd_s.at[0, k], 3)
            c.start()
            sends.append(c)
        c = send(up_col, k, sibling, fwd_s.at[2, k], 5)
        c.start()
        sends.append(c)

    def relay_far(k):
        recv(far_col, k, 3)
        c = send(far_col, k, sibling, fwd_s.at[3, k], 6)
        c.start()
        sends.append(c)

    ut_c.wait()
    us_c.wait()
    picks = lax.broadcasted_iota(jnp.int32, (64, 254), 0)
    cluster = lax.broadcasted_iota(jnp.int32, (64, 254), 1)
    want = jnp.where(picks < 8, row * 8 + picks, -1)
    want = jnp.where((picks >= 8) & (picks < 12), 128 + row * 4 + picks - 8, want)
    want = jnp.where((picks >= 12) & (picks < 14), 192 + row * 2 + picks - 12, want)
    want = jnp.where((picks >= 16) & (picks < 46), 224 + picks - 16, want)
    for j in range(7):
        want = jnp.where(picks == 48 + j, 256 - (256 >> j) + (device // (1 << j)), want)
    pick_u = (cluster == want).astype(BF16)
    picks_s = lax.broadcasted_iota(jnp.int32, (16, 254), 0)
    cluster_s = lax.broadcasted_iota(jnp.int32, (16, 254), 1)
    want_s = jnp.full((16, 254), -1, jnp.int32)
    for j in range(7):
        want_s = jnp.where(picks_s == j, 256 - (256 >> j) + (device // (1 << j)), want_s)
    pick_s = (cluster_s == want_s).astype(BF16)

    def turn_upper(q, carry):
        w = jnp.concatenate([ut[q], ut[q + 32]], axis=0)
        mu[pl.ds(q, 64, stride=32), :] = dot_nt(pick_u, w)
        return carry

    lax.fori_loop(0, 32, turn_upper, 0, unroll=2)

    def unpack_upper(g, carry):
        for u in range(8):
            unpack(mu, eu, g * 8 + u)
        return carry

    lax.fori_loop(0, 8, unpack_upper, 0)

    def turn_sib(q, carry):
        w = jnp.concatenate([us[q], us[q + 32]], axis=0)
        mp[pl.ds(q, 16, stride=32), :] = dot_nt(pick_s, w)
        return carry

    lax.fori_loop(0, 32, turn_sib, 0, unroll=2)

    def unpack_sib(g, carry):
        for u in range(8):
            unpack(mp, su, g * 8 + u)
        return carry

    lax.fori_loop(0, 1, unpack_sib, 0)

    relay_near(0)

    for i in range(1, COLS):
        peer = lax.rem(col + COLS - i, COLS)
        pltpu.make_async_remote_copy(
            xr.at[peer], xr.at[peer], xr_s.at[i], xr_r.at[i],
            device_id=(row, peer), device_id_type=MESH).wait_recv()
    for i in range(4):
        upair[i] = xr[2 * i] + xr[2 * i + 1]

    def up_upper(source, count, target, first):
        for i in range(count // 2):
            one = lift(upair[source + 2 * i], eu[first + 4 * i : first + 4 * i + 2])
            two = lift(upair[source + 2 * i + 1], eu[first + 4 * i + 2 : first + 4 * i + 4])
            upair[target + i] = jnp.concatenate([one, two], axis=1)

    up_upper(0, 4, 4, 0)
    up_upper(4, 2, 6, 8)
    row_root = lift(upair[6], eu[12:14])
    zr[row] = placed(row_root, lax.rem(row, 2))
    zr_copies = []
    for i in range(1, ROWS):
        c = pltpu.make_async_remote_copy(
            zr.at[row], zr.at[row], zr_s.at[i], zr_r.at[i],
            device_id=(lax.rem(row + i, ROWS), col), device_id_type=MESH)
        c.start()
        zr_copies.append(c)

    relay_near(1)

    halo_next.wait_recv()
    halo_prev.wait_recv()
    eh[0] = split(halo[0])
    eh[LEAVES + 1] = split(halo[1])
    leaf_first = device * LEAVES

    def near_part(k):
        nb_c[k].wait()

        def near_step(g, carry):
            for u in range(4):
                s = k * per + g * 4 + u
                source = jnp.clip(nsrc[s] - leaf_first + 1, 0, LEAVES + 1)
                o = dot_nt(eh[source], nb[s])
                prod[pl.ds(s, RHS, stride=SLOTS), :] = joined(o)
            return carry

        lax.fori_loop(0, per // 4, near_step, 0)

    near_part(0)
    near_part(1)
    relay_near(2)
    near_part(2)

    ls_c.wait()
    for h in range(1, HEIGHT):
        count = PAIRS >> h

        def sib_one(p, h=h):
            x = lev[lev_base(h) + p]
            lhs = jnp.concatenate([split(x[:, 64:]), split(x[:, :64])], axis=0)
            w = ls[pl.ds(LEAVES - 2 * (LEAVES >> h) + 2 * p, 2)].reshape(128, 64)
            o = dot_nt(lhs, w)
            sib[lev_base(h) + p] = jnp.where(first_half, o[0:16] + o[16:32], o[32:48] + o[48:64])

        group = min(count, 4)

        def sib_step(g, carry, sib_one=sib_one, group=group):
            for u in range(group):
                sib_one(g * group + u)
            return carry

        lax.fori_loop(0, count // group, sib_step, 0)

    relay_near(3)

    for i in range(1, ROWS):
        peer = lax.rem(row + ROWS - i, ROWS)
        pltpu.make_async_remote_copy(
            zr.at[peer], zr.at[peer], zr_s.at[i], zr_r.at[i],
            device_id=(peer, col), device_id_type=MESH).wait_recv()
    for i in range(8):
        upair[7 + i] = zr[2 * i] + zr[2 * i + 1]
    up_upper(7, 8, 15, 16)
    up_upper(15, 4, 19, 32)
    up_upper(19, 2, 21, 40)

    own = []
    for j, base in enumerate((0, 4, 6, 7, 15, 19, 21)):
        own.append((base, col // (1 << j)) if j < 3 else (base, row // (1 << (j - 3))))
    y = jnp.zeros((RHS, RANK), F32)
    for j in range(6, -1, -1):
        base, mine = own[j]
        pair = upair[base + mine // 2]
        turned = jnp.concatenate([pair[:, 64:], pair[:, :64]], axis=1)
        other = jnp.where(lax.rem(mine, 2) == 1, pair, turned)[:, :64]
        y = joined(dot_nt(split(other), su[j])) + joined(dot_nt(split(y), eu[48 + j]))

    ylev[30] = placed(y, 0)
    for h in range(HEIGHT - 1, -1, -1):
        count = PAIRS >> h
        off = level_offset(h)

        def down_one(parent, p, h=h, off=off):
            w = mb[pl.ds(off + 2 * p, 2)].reshape(128, 64)
            value = joined(dot_nt(split(parent), w))
            if h:
                ylev[lev_base(h) + p] = value + sib[lev_base(h) + p]
            else:
                carried[p] = value

        if h == HEIGHT - 1:
            down_one(y, 0)
            continue

        def down_two(q, h=h, down_one=down_one):
            pair = ylev[lev_base(h + 1) + q]
            down_one(pair[:, :64], 2 * q)
            down_one(pair[:, 64:], 2 * q + 1)

        half = count // 2
        group = min(half, 4)

        def down_step(g, carry, down_two=down_two, group=group):
            for u in range(group):
                down_two(g * group + u)
            return carry

        lax.fori_loop(0, half // group, down_step, 0)

    lc_c.wait()

    def pack_leaf(g, carry):
        for u in range(4):
            t = g * 4 + u
            cp[t] = jnp.concatenate([lc[t, 0], lc[t, 1], lc[t, 2], lc[t, 3]], axis=1)
        return carry

    lax.fori_loop(0, LEAVES // 4, pack_leaf, 0)

    near_part(3)

    target = nt_v[...] - leaf_first
    slot = lax.broadcasted_iota(jnp.int32, (LEAVES, SLOTS), 1)
    one_hot = (
        (jnp.broadcast_to(target, (LEAVES, SLOTS))
         == lax.broadcasted_iota(jnp.int32, (LEAVES, SLOTS), 0))
        & (slot < ncnt[0])
    ).astype(BF16)

    def sum_step(g, carry):
        for u in range(2):
            r = g * 2 + u
            x = prod[pl.ds(pl.multiple_of(r * SLOTS, SLOTS), SLOTS), :]
            high = x.astype(BF16)
            low = (x - high.astype(F32)).astype(BF16)
            nacc[pl.ds(r, LEAVES, stride=RHS), :] = dot_nn(one_hot, high) + dot_nn(one_hot, low)
        return carry

    lax.fori_loop(0, RHS // 2, sum_step, 0)

    def dup_part(owner, k):
        def dup_step(g, carry):
            for u in range(4):
                p = k * PART + g * 4 + u
                x = gath[owner, p]
                turned = jnp.concatenate([x[:, 64:], x[:, :64]], axis=1)
                base = owner * LEAVES + 2 * p
                dup[base] = split(jnp.where(first_half, x, turned))
                dup[base + 1] = split(jnp.where(first_half, turned, x))
            return carry

        lax.fori_loop(0, PART // 4, dup_step, 0)

    for k in range(CHUNKS):
        relay_far(k)
    other = 1 - core
    for k in range(CHUNKS):
        dup_part(col, k)
        dup_part(down_col, k)
        dup_part(up_col, k)
        recv(sibling, k, 0)
        dup_part(sibling, k)
        recv(zprev * 2 + other, k, 4)
        dup_part(zprev * 2 + other, k)
        recv(znext * 2 + other, k, 5)
        dup_part(znext * 2 + other, k)
    for k in range(CHUNKS):
        dup_part(far_col, k)
        recv(zfar * 2 + other, k, 6)
        dup_part(zfar * 2 + other, k)

    bt_c.wait()
    group_first = row * (LEAVES * COLS)

    def final_leaf(t, q, u):
        d = [dup[jnp.clip(lsrc[j, t] - group_first, 0, LEAVES * COLS - 1)] for j in range(PARTNERS)]
        lhs = jnp.concatenate(
            [jnp.where(first_half2, d[0], d[1]), jnp.where(first_half2, d[2], d[3])], axis=1)
        c = carried[q]
        c = c[:, :64] if u == 0 else c[:, 64:]
        y0 = joined(dot_nt(lhs, cp[t])) + c
        start = pl.multiple_of(t * LEAF, LEAF)
        far = joined(dot_nn(split(y0), bt[:, pl.ds(start, LEAF)]))
        out[:, pl.ds(start, LEAF)] = far + nacc[pl.ds(pl.multiple_of(t * RHS, RHS), RHS), :]

    def final_step(g, carry):
        for u in range(4):
            q = g * 4 + u
            final_leaf(2 * q, q, 0)
            final_leaf(2 * q + 1, q, 1)
        return carry

    lax.fori_loop(0, PAIRS // 4, final_step, 0)
    out_c = pltpu.make_async_copy(out, out_h, out_sem)
    out_c.start()
    halo_next.wait_send()
    halo_prev.wait_send()
    for c in sends + xr_copies + zr_copies:
        c.wait_send()
    out_c.wait()


def shards(
    emission, basis_source, basis_target, local_transfer, local_sibling, upper_transfer,
    upper_sibling, leaf_source, leaf_coupling, near_block, near_target, near_source, near_count,
):
    hbm = pl.BlockSpec(memory_space=pl.ANY)
    smem = pl.BlockSpec(memory_space=pltpu.SMEM)
    vmem = pl.BlockSpec(memory_space=pltpu.VMEM)
    dma = pltpu.SemaphoreType.DMA
    V = pltpu.VMEM
    return pl.pallas_call(
        kernel,
        out_shape=jax.ShapeDtypeStruct((RHS, LEAVES * LEAF), F32),
        in_specs=[hbm] * 7 + [smem, hbm, hbm, vmem, smem, smem],
        out_specs=hbm,
        scratch_shapes=[
            V((RHS, 8192), F32), V((RANK, 8192), BF16), V((RANK, 8192), BF16),
            V((64, 64, 126), BF16), V((62, 64, 64), BF16),
            V((64, 64, 254), BF16), V((64, 64, 254), BF16),
            V((LEAVES, PARTNERS, 64, 64), BF16), V((SLOTS, 128, 128), BF16),
            V((LEAVES + 2, 32, 128), BF16),
            V((2, RHS, 128), F32),
            V((COLS, PAIRS, RHS, 128), F32),
            V((COLS * LEAVES, 32, 128), BF16),
            V((128 * 32, 128), F32),
            V((126, 64, 64), BF16),
            V((64 * 32, 128), F32),
            V((64, 64, 64), BF16),
            V((8, 64, 64), BF16),
            V((32, RHS, 128), F32),
            V((32, RHS, 128), F32),
            V((32, RHS, 128), F32),
            V((PAIRS, RHS, 128), F32),
            V((COLS, RHS, 128), F32),
            V((ROWS, RHS, 128), F32),
            V((22, RHS, 128), F32),
            V((RHS * SLOTS, 128), F32),
            V((LEAVES * RHS, 128), F32),
            V((LEAVES, 64, 256), BF16),
            V((RHS, 8192), F32),
            dma((7,)), dma((NEAR_PARTS,)), dma((CHUNKS,)), dma, dma((2,)), dma((2,)),
            dma((3, CHUNKS)), dma((4, CHUNKS)), dma((7, CHUNKS)),
            dma((COLS,)), dma((COLS,)), dma((ROWS,)), dma((ROWS,)),
        ],
        compiler_params=pltpu.CompilerParams(
            collective_id=0, has_side_effects=True, vmem_limit_bytes=58 * 1024 * 1024),
        name="h2_product",
    )(
        emission, basis_source, basis_target, local_transfer.transpose(1, 2, 0), local_sibling,
        upper_transfer.transpose(1, 2, 0), upper_sibling.transpose(1, 2, 0), leaf_source.T,
        leaf_coupling, near_block, near_target.reshape(1, SLOTS), near_source, near_count,
    )


def solution(mesh):
    both = ("row", "col")
    in_specs = (
        P(None, both), P(None, both), P(None, both), P(both, None, None), P(both, None, None),
        P(), P(), P(both, None), P(both, None, None, None), P(both, None, None),
        P(both), P(both), P(both),
    )
    return jax.shard_map(
        shards, mesh=mesh, in_specs=in_specs, out_specs=P(None, both), check_vma=False)
```

```python
import functools

import jax
import jax.numpy as jnp
from jax import lax
from jax.experimental import pallas as pl
from jax.experimental.pallas import tpu as pltpu
from jax.sharding import PartitionSpec as P

MESH = pl.DeviceIdType.MESH
F32 = jnp.float32
BF16 = jnp.bfloat16

RHS = 16
RANK = 64
LEAF = 128
LEAVES = 64
PAIRS = LEAVES // 2
PARTNERS = 4
SLOTS = 192
ROWS, COLS = 16, 8
CHUNKS = 4
PART = PAIRS // CHUNKS
HEIGHT = 6
NEAR_PARTS = 4
FINAL = 16


def dot_nn(a, b):
    return lax.dot_general(a, b, (((1,), (0,)), ((), ())), preferred_element_type=F32)


def dot_nt(a, b):
    return lax.dot_general(a, b, (((1,), (1,)), ((), ())), preferred_element_type=F32)


def split(x):
    high = x.astype(BF16)
    low = (x - high.astype(F32)).astype(BF16)
    return jnp.concatenate([high, low], axis=0)


def joined(o):
    half = o.shape[0] // 2
    return o[:half] + o[half:]


def level_offset(h):
    return 2 * LEAVES - 2 * (LEAVES >> h)


def lev_base(h):
    return PAIRS - (PAIRS >> (h - 1)) if h >= 1 else 0


def kernel(
    em_h, bs_h, bt_h, lt_h, ls_h, ut_h, us_h, lsrc, lc_h, nb_h, nt_v, nsrc, ncnt,
    out_h,
    em, bs, bt, lt, ls, ut, us, lc, nb,
    eh, halo, gath, dup, mp, mb, mu, eu, su, lev, sib, ylev, carried,
    xr, zr, upair, prod, nacc, cp, out,
    load_sem, nb_sem, bs_sem, out_sem, halo_s, halo_r,
    own_s, fwd_s, gath_r, xr_s, xr_r, zr_s, zr_r,
):
    row, col = lax.axis_index("row"), lax.axis_index("col")
    device = row * COLS + col
    z, core = col // 2, col % 2
    sibling = z * 2 + 1 - core
    znext = lax.rem(z + 1, 4)
    zprev = lax.rem(z + 3, 4)
    zfar = lax.rem(z + 2, 4)
    up_col, down_col, far_col = znext * 2 + core, zprev * 2 + core, zfar * 2 + core

    def load(src, dst, i):
        c = pltpu.make_async_copy(src, dst, load_sem.at[i])
        c.start()
        return c

    em_c = load(em_h, em, 0)
    width = 8192 // CHUNKS
    bs_c = []
    for k in range(CHUNKS):
        c = pltpu.make_async_copy(
            bs_h.at[:, pl.ds(k * width, width)], bs.at[:, pl.ds(k * width, width)], bs_sem.at[k]
        )
        c.start()
        bs_c.append(c)
    lt_c = load(lt_h, lt, 1)

    barrier = pltpu.get_barrier_semaphore()
    nxt, prv = lax.rem(device + 1, ROWS * COLS), lax.rem(device + ROWS * COLS - 1, ROWS * COLS)
    next_id = (nxt // COLS, lax.rem(nxt, COLS))
    prev_id = (prv // COLS, lax.rem(prv, COLS))
    for i in range(1, COLS):
        pl.semaphore_signal(barrier, 1, device_id=(row, lax.rem(col + i, COLS)), device_id_type=MESH)
    for i in range(1, ROWS):
        pl.semaphore_signal(barrier, 1, device_id=(lax.rem(row + i, ROWS), col), device_id_type=MESH)
    pl.semaphore_signal(barrier, 1, device_id=next_id, device_id_type=MESH)
    pl.semaphore_signal(barrier, 1, device_id=prev_id, device_id_type=MESH)

    ut_c = load(ut_h, ut, 2)
    us_c = load(us_h, us, 3)
    ls_c = load(ls_h, ls, 4)
    nb_c = []
    per = SLOTS // NEAR_PARTS
    for k in range(NEAR_PARTS):
        c = pltpu.make_async_copy(
            nb_h.at[pl.ds(k * per, per)], nb.at[pl.ds(k * per, per)], nb_sem.at[k]
        )
        c.start()
        nb_c.append(c)
    lc_c = load(lc_h, lc, 5)
    bt_c = load(bt_h, bt, 6)

    lane = lax.broadcasted_iota(jnp.int32, (RHS, 128), 1)
    first_half = lane < 64
    lane2 = lax.broadcasted_iota(jnp.int32, (2 * RHS, 128), 1)
    first_half2 = lane2 < 64

    em_c.wait()

    def split_leaf(g, carry):
        for u in range(8):
            l = g * 8 + u
            eh[l + 1] = split(em[:, pl.ds(pl.multiple_of(l * LEAF, LEAF), LEAF)])
        return carry

    lax.fori_loop(0, LEAVES // 8, split_leaf, 0)

    pl.semaphore_wait(barrier, COLS - 1 + ROWS - 1 + 2)

    halo_next = pltpu.make_async_remote_copy(
        em.at[:, pl.ds((LEAVES - 1) * LEAF, LEAF)], halo.at[0], halo_s.at[0], halo_r.at[0],
        device_id=next_id, device_id_type=MESH)
    halo_prev = pltpu.make_async_remote_copy(
        em.at[:, pl.ds(0, LEAF)], halo.at[1], halo_s.at[1], halo_r.at[1],
        device_id=prev_id, device_id_type=MESH)
    halo_next.start()
    halo_prev.start()

    def piece(owner, k):
        return gath.at[owner, pl.ds(k * PART, PART)]

    def send(owner, k, to_col, send_sem, kind):
        return pltpu.make_async_remote_copy(
            piece(owner, k), piece(owner, k), send_sem, gath_r.at[kind, k],
            device_id=(row, to_col), device_id_type=MESH)

    sends = []

    def leaf_pair(p):
        a = eh[pl.ds(2 * p + 1, 2)].reshape(64, 128)
        start = pl.multiple_of(p * 256, 256)
        w = bs[:, pl.ds(start, 256)]
        b = jnp.concatenate([w[:, :128], w[:, 128:]], axis=0)
        o = dot_nt(a, b)
        gath[col, p] = jnp.where(first_half, o[0:16] + o[16:32], o[32:48] + o[48:64])

    for k in range(CHUNKS):
        bs_c[k].wait()

        def leaf_step(g, carry, k=k):
            for u in range(8):
                leaf_pair(k * PART + g * 8 + u)
            return carry

        lax.fori_loop(0, PART // 8, leaf_step, 0)
        for n, (to_col, kind) in enumerate(((up_col, 1), (down_col, 2), (sibling, 0))):
            c = send(col, k, to_col, own_s.at[n, k], kind)
            c.start()
            sends.append(c)

    lt_c.wait()
    eye = (
        lax.broadcasted_iota(jnp.int32, (128, 126), 0)
        == lax.broadcasted_iota(jnp.int32, (128, 126), 1)
    ).astype(BF16)

    def turn_local(q, carry):
        w = jnp.concatenate([lt[q], lt[q + 32]], axis=0)
        mp[pl.ds(q, 128, stride=32), :] = dot_nt(eye, w)
        return carry

    lax.fori_loop(0, 32, turn_local, 0, unroll=4)

    def unpack(source, target, n):
        m = source[pl.ds(pl.multiple_of(n * 32, 32), 32), :].astype(BF16)
        target[n] = jnp.concatenate([m[:, :64], m[:, 64:]], axis=0)

    def unpack_local(g, carry):
        for u in range(18):
            unpack(mp, mb, g * 18 + u)
        return carry

    lax.fori_loop(0, 7, unpack_local, 0)

    def lift(pair, weights):
        return joined(dot_nn(split(pair), weights.reshape(128, 64)))

    def level_pair(h, p):
        return gath[col, p] if h == 0 else lev[lev_base(h) + p]

    for h in range(HEIGHT - 1):
        count = PAIRS >> h
        off = level_offset(h)

        def up_two(q, h=h, off=off):
            one = lift(level_pair(h, 2 * q), mb[pl.ds(off + 4 * q, 2)])
            two = lift(level_pair(h, 2 * q + 1), mb[pl.ds(off + 4 * q + 2, 2)])
            lev[lev_base(h + 1) + q] = jnp.concatenate([one, two], axis=1)

        half = count // 2
        group = min(half, 8)

        def up_step(g, carry, up_two=up_two, group=group):
            for u in range(group):
                up_two(g * group + u)
            return carry

        lax.fori_loop(0, half // group, up_step, 0)
    root = lift(lev[lev_base(5)], mb[pl.ds(level_offset(5), 2)])

    def placed(value, parity):
        return jnp.where(
            (lane >= 64).astype(jnp.int32) == parity, jnp.concatenate([value, value], axis=1), 0.0
        )

    xr[col] = placed(root, core)
    xr_copies = []
    for i in range(1, COLS):
        c = pltpu.make_async_remote_copy(
            xr.at[col], xr.at[col], xr_s.at[i], xr_r.at[i],
            device_id=(row, lax.rem(col + i, COLS)), device_id_type=MESH)
        c.start()
        xr_copies.append(c)

    def recv(owner, k, kind):
        pltpu.make_async_remote_copy(
            piece(owner, k), piece(owner, k), own_s.at[0, k], gath_r.at[kind, k],
            device_id=(row, col), device_id_type=MESH).wait_recv()

    def relay_near(k):
        recv(down_col, k, 1)
        if k < CHUNKS // 2:
            c = send(down_col, k, up_col, fwd_s.at[0, k], 3)
            c.start()
            sends.append(c)
        c = send(down_col, k, sibling, fwd_s.at[1, k], 4)
        c.start()
        sends.append(c)
        recv(up_col, k, 2)
        if k >= CHUNKS // 2:
            c = send(up_col, k, down_col, fwd_s.at[0, k], 3)
            c.start()
            sends.append(c)
        c = send(up_col, k, sibling, fwd_s.at[2, k], 5)
        c.start()
        sends.append(c)

    def relay_far(k):
        recv(far_col, k, 3)
        c = send(far_col, k, sibling, fwd_s.at[3, k], 6)
        c.start()
        sends.append(c)

    ut_c.wait()
    us_c.wait()
    picks = lax.broadcasted_iota(jnp.int32, (64, 254), 0)
    cluster = lax.broadcasted_iota(jnp.int32, (64, 254), 1)
    want = jnp.where(picks < 8, row * 8 + picks, -1)
    want = jnp.where((picks >= 8) & (picks < 12), 128 + row * 4 + picks - 8, want)
    want = jnp.where((picks >= 12) & (picks < 14), 192 + row * 2 + picks - 12, want)
    want = jnp.where((picks >= 16) & (picks < 46), 224 + picks - 16, want)
    for j in range(7):
        want = jnp.where(picks == 48 + j, 256 - (256 >> j) + (device // (1 << j)), want)
    pick_u = (cluster == want).astype(BF16)
    picks_s = lax.broadcasted_iota(jnp.int32, (16, 254), 0)
    cluster_s = lax.broadcasted_iota(jnp.int32, (16, 254), 1)
    want_s = jnp.full((16, 254), -1, jnp.int32)
    for j in range(7):
        want_s = jnp.where(picks_s == j, 256 - (256 >> j) + (device // (1 << j)), want_s)
    pick_s = (cluster_s == want_s).astype(BF16)

    def turn_upper(q, carry):
        w = jnp.concatenate([ut[q], ut[q + 32]], axis=0)
        mu[pl.ds(q, 64, stride=32), :] = dot_nt(pick_u, w)
        w = jnp.concatenate([us[q], us[q + 32]], axis=0)
        mp[pl.ds(q, 16, stride=32), :] = dot_nt(pick_s, w)
        return carry

    lax.fori_loop(0, 32, turn_upper, 0, unroll=4)

    def unpack_upper(g, carry):
        for u in range(16):
            unpack(mu, eu, g * 16 + u)
        for u in range(2):
            unpack(mp, su, g * 2 + u)
        return carry

    lax.fori_loop(0, 4, unpack_upper, 0)

    relay_near(0)

    for i in range(1, COLS):
        peer = lax.rem(col + COLS - i, COLS)
        pltpu.make_async_remote_copy(
            xr.at[peer], xr.at[peer], xr_s.at[i], xr_r.at[i],
            device_id=(row, peer), device_id_type=MESH).wait_recv()
    for i in range(4):
        upair[i] = xr[2 * i] + xr[2 * i + 1]

    def up_upper(source, count, target, first):
        for i in range(count // 2):
            one = lift(upair[source + 2 * i], eu[first + 4 * i : first + 4 * i + 2])
            two = lift(upair[source + 2 * i + 1], eu[first + 4 * i + 2 : first + 4 * i + 4])
            upair[target + i] = jnp.concatenate([one, two], axis=1)

    up_upper(0, 4, 4, 0)
    up_upper(4, 2, 6, 8)
    row_root = lift(upair[6], eu[12:14])
    zr[row] = placed(row_root, lax.rem(row, 2))
    zr_copies = []
    for i in range(1, ROWS):
        c = pltpu.make_async_remote_copy(
            zr.at[row], zr.at[row], zr_s.at[i], zr_r.at[i],
            device_id=(lax.rem(row + i, ROWS), col), device_id_type=MESH)
        c.start()
        zr_copies.append(c)

    relay_near(1)

    halo_next.wait_recv()
    halo_prev.wait_recv()
    eh[0] = split(halo[0])
    eh[LEAVES + 1] = split(halo[1])
    leaf_first = device * LEAVES

    def near_part(k):
        nb_c[k].wait()

        def near_step(g, carry):
            for u in range(16):
                s = k * per + g * 16 + u
                source = jnp.clip(nsrc[s] - leaf_first + 1, 0, LEAVES + 1)
                o = dot_nt(eh[source], nb[s])
                prod[pl.ds(s, RHS, stride=SLOTS), :] = joined(o)
            return carry

        lax.fori_loop(0, per // 16, near_step, 0)

    near_part(0)
    near_part(1)
    relay_near(2)
    near_part(2)

    ls_c.wait()
    for h in range(1, HEIGHT):
        count = PAIRS >> h

        def sib_one(p, h=h):
            x = lev[lev_base(h) + p]
            lhs = jnp.concatenate([split(x[:, 64:]), split(x[:, :64])], axis=0)
            w = ls[pl.ds(LEAVES - 2 * (LEAVES >> h) + 2 * p, 2)].reshape(128, 64)
            o = dot_nt(lhs, w)
            sib[lev_base(h) + p] = jnp.where(first_half, o[0:16] + o[16:32], o[32:48] + o[48:64])

        group = min(count, 8)

        def sib_step(g, carry, sib_one=sib_one, group=group):
            for u in range(group):
                sib_one(g * group + u)
            return carry

        lax.fori_loop(0, count // group, sib_step, 0)

    relay_near(3)

    for i in range(1, ROWS):
        peer = lax.rem(row + ROWS - i, ROWS)
        pltpu.make_async_remote_copy(
            zr.at[peer], zr.at[peer], zr_s.at[i], zr_r.at[i],
            device_id=(peer, col), device_id_type=MESH).wait_recv()
    for i in range(8):
        upair[7 + i] = zr[2 * i] + zr[2 * i + 1]
    up_upper(7, 8, 15, 16)
    up_upper(15, 4, 19, 32)
    up_upper(19, 2, 21, 40)

    own = []
    for j, base in enumerate((0, 4, 6, 7, 15, 19, 21)):
        own.append((base, col // (1 << j)) if j < 3 else (base, row // (1 << (j - 3))))
    y = jnp.zeros((RHS, RANK), F32)
    for j in range(6, -1, -1):
        base, mine = own[j]
        pair = upair[base + mine // 2]
        turned = jnp.concatenate([pair[:, 64:], pair[:, :64]], axis=1)
        other = jnp.where(lax.rem(mine, 2) == 1, pair, turned)[:, :64]
        y = joined(dot_nt(split(other), su[j])) + joined(dot_nt(split(y), eu[48 + j]))

    ylev[30] = placed(y, 0)
    for h in range(HEIGHT - 1, -1, -1):
        count = PAIRS >> h
        off = level_offset(h)

        def down_one(parent, p, h=h, off=off):
            w = mb[pl.ds(off + 2 * p, 2)].reshape(128, 64)
            value = joined(dot_nt(split(parent), w))
            if h:
                ylev[lev_base(h) + p] = value + sib[lev_base(h) + p]
            else:
                carried[p] = value

        if h == HEIGHT - 1:
            down_one(y, 0)
            continue

        def down_two(q, h=h, down_one=down_one):
            pair = ylev[lev_base(h + 1) + q]
            down_one(pair[:, :64], 2 * q)
            down_one(pair[:, 64:], 2 * q + 1)

        half = count // 2
        group = min(half, 8)

        def down_step(g, carry, down_two=down_two, group=group):
            for u in range(group):
                down_two(g * group + u)
            return carry

        lax.fori_loop(0, half // group, down_step, 0)

    lc_c.wait()

    def pack_leaf(g, carry):
        for u in range(16):
            t = g * 16 + u
            cp[t] = jnp.concatenate([lc[t, 0], lc[t, 1], lc[t, 2], lc[t, 3]], axis=1)
        return carry

    lax.fori_loop(0, LEAVES // 16, pack_leaf, 0)

    near_part(3)

    target = nt_v[...] - leaf_first
    slot = lax.broadcasted_iota(jnp.int32, (LEAVES, SLOTS), 1)
    one_hot = (
        (jnp.broadcast_to(target, (LEAVES, SLOTS))
         == lax.broadcasted_iota(jnp.int32, (LEAVES, SLOTS), 0))
        & (slot < ncnt[0])
    ).astype(BF16)

    def sum_step(g, carry):
        for u in range(4):
            r = g * 4 + u
            x = prod[pl.ds(pl.multiple_of(r * SLOTS, SLOTS), SLOTS), :]
            high = x.astype(BF16)
            low = (x - high.astype(F32)).astype(BF16)
            nacc[pl.ds(r, LEAVES, stride=RHS), :] = dot_nn(one_hot, high) + dot_nn(one_hot, low)
        return carry

    lax.fori_loop(0, RHS // 4, sum_step, 0)

    def dup_part(owner, k):
        def dup_step(g, carry):
            for u in range(8):
                p = k * PART + g * 8 + u
                x = gath[owner, p]
                turned = jnp.concatenate([x[:, 64:], x[:, :64]], axis=1)
                base = owner * LEAVES + 2 * p
                dup[base] = split(jnp.where(first_half, x, turned))
                dup[base + 1] = split(jnp.where(first_half, turned, x))
            return carry

        lax.fori_loop(0, PART // 8, dup_step, 0)

    for k in range(CHUNKS):
        relay_far(k)
    other = 1 - core
    for k in range(CHUNKS):
        dup_part(col, k)
        dup_part(down_col, k)
        dup_part(up_col, k)
        recv(sibling, k, 0)
        dup_part(sibling, k)
        recv(zprev * 2 + other, k, 4)
        dup_part(zprev * 2 + other, k)
        recv(znext * 2 + other, k, 5)
        dup_part(znext * 2 + other, k)
    for k in range(CHUNKS):
        dup_part(far_col, k)
        recv(zfar * 2 + other, k, 6)
        dup_part(zfar * 2 + other, k)

    bt_c.wait()
    group_first = row * (LEAVES * COLS)

    def final_step(g, carry):
        leaves = [g * FINAL + u for u in range(FINAL)]
        lhs = []
        for t in leaves:
            d = [dup[jnp.clip(lsrc[j, t] - group_first, 0, LEAVES * COLS - 1)]
                 for j in range(PARTNERS)]
            lhs.append(jnp.concatenate(
                [jnp.where(first_half2, d[0], d[1]), jnp.where(first_half2, d[2], d[3])], axis=1))
        listed = [dot_nt(x, cp[t]) for x, t in zip(lhs, leaves)]
        y0 = []
        for u, o in enumerate(listed):
            c = carried[g * (FINAL // 2) + u // 2]
            y0.append(split(joined(o) + (c[:, :64] if u % 2 == 0 else c[:, 64:])))
        starts = [pl.multiple_of(t * LEAF, LEAF) for t in leaves]
        far = [dot_nn(y, bt[:, pl.ds(start, LEAF)]) for y, start in zip(y0, starts)]
        for o, t, start in zip(far, leaves, starts):
            near = nacc[pl.ds(pl.multiple_of(t * RHS, RHS), RHS), :]
            out[:, pl.ds(start, LEAF)] = joined(o) + near
        return carry

    lax.fori_loop(0, LEAVES // FINAL, final_step, 0)
    out_c = pltpu.make_async_copy(out, out_h, out_sem)
    out_c.start()
    halo_next.wait_send()
    halo_prev.wait_send()
    for c in sends + xr_copies + zr_copies:
        c.wait_send()
    out_c.wait()


def shards(
    emission, basis_source, basis_target, local_transfer, local_sibling, upper_transfer,
    upper_sibling, leaf_source, leaf_coupling, near_block, near_target, near_source, near_count,
):
    hbm = pl.BlockSpec(memory_space=pl.ANY)
    smem = pl.BlockSpec(memory_space=pltpu.SMEM)
    vmem = pl.BlockSpec(memory_space=pltpu.VMEM)
    dma = pltpu.SemaphoreType.DMA
    V = pltpu.VMEM
    return pl.pallas_call(
        kernel,
        out_shape=jax.ShapeDtypeStruct((RHS, LEAVES * LEAF), F32),
        in_specs=[hbm] * 7 + [smem, hbm, hbm, vmem, smem, smem],
        out_specs=hbm,
        scratch_shapes=[
            V((RHS, 8192), F32), V((RANK, 8192), BF16), V((RANK, 8192), BF16),
            V((64, 64, 126), BF16), V((62, 64, 64), BF16),
            V((64, 64, 254), BF16), V((64, 64, 254), BF16),
            V((LEAVES, PARTNERS, 64, 64), BF16), V((SLOTS, 128, 128), BF16),
            V((LEAVES + 2, 32, 128), BF16),
            V((2, RHS, 128), F32),
            V((COLS, PAIRS, RHS, 128), F32),
            V((COLS * LEAVES, 32, 128), BF16),
            V((128 * 32, 128), F32),
            V((126, 64, 64), BF16),
            V((64 * 32, 128), F32),
            V((64, 64, 64), BF16),
            V((8, 64, 64), BF16),
            V((32, RHS, 128), F32),
            V((32, RHS, 128), F32),
            V((32, RHS, 128), F32),
            V((PAIRS, RHS, 128), F32),
            V((COLS, RHS, 128), F32),
            V((ROWS, RHS, 128), F32),
            V((22, RHS, 128), F32),
            V((RHS * SLOTS, 128), F32),
            V((LEAVES * RHS, 128), F32),
            V((LEAVES, 64, 256), BF16),
            V((RHS, 8192), F32),
            dma((7,)), dma((NEAR_PARTS,)), dma((CHUNKS,)), dma, dma((2,)), dma((2,)),
            dma((3, CHUNKS)), dma((4, CHUNKS)), dma((7, CHUNKS)),
            dma((COLS,)), dma((COLS,)), dma((ROWS,)), dma((ROWS,)),
        ],
        compiler_params=pltpu.CompilerParams(
            collective_id=0, has_side_effects=True, vmem_limit_bytes=58 * 1024 * 1024),
        name="h2_product",
    )(
        emission, basis_source, basis_target, local_transfer.transpose(1, 2, 0), local_sibling,
        upper_transfer.transpose(1, 2, 0), upper_sibling.transpose(1, 2, 0), leaf_source.T,
        leaf_coupling, near_block, near_target.reshape(1, SLOTS), near_source, near_count,
    )


def solution(mesh):
    both = ("row", "col")
    in_specs = (
        P(None, both), P(None, both), P(None, both), P(both, None, None), P(both, None, None),
        P(), P(), P(both, None), P(both, None, None, None), P(both, None, None),
        P(both), P(both), P(both),
    )
    return jax.shard_map(
        shards, mesh=mesh, in_specs=in_specs, out_specs=P(None, both), check_vma=False)
```

```python
import functools

import jax
import jax.numpy as jnp
from jax import lax
from jax.experimental import pallas as pl
from jax.experimental.pallas import tpu as pltpu
from jax.sharding import PartitionSpec as P

MESH = pl.DeviceIdType.MESH
F32 = jnp.float32
BF16 = jnp.bfloat16

RHS = 16
RANK = 64
LEAF = 128
LEAVES = 64
PAIRS = LEAVES // 2
PARTNERS = 4
SLOTS = 192
ROWS, COLS = 16, 8
CHUNKS = 4
PART = PAIRS // CHUNKS
HEIGHT = 6
NEAR_PARTS = 4
FINAL = 16
MAT, SLOT_ROWS, LEAF_ROWS = 33, SLOTS + 1, RHS + 1


def dot_nn(a, b):
    return lax.dot_general(a, b, (((1,), (0,)), ((), ())), preferred_element_type=F32)


def dot_nt(a, b):
    return lax.dot_general(a, b, (((1,), (1,)), ((), ())), preferred_element_type=F32)


def split(x):
    high = x.astype(BF16)
    low = (x - high.astype(F32)).astype(BF16)
    return jnp.concatenate([high, low], axis=0)


def joined(o):
    half = o.shape[0] // 2
    return o[:half] + o[half:]


def level_offset(h):
    return 2 * LEAVES - 2 * (LEAVES >> h)


def lev_base(h):
    return PAIRS - (PAIRS >> (h - 1)) if h >= 1 else 0


def kernel(
    em_h, bs_h, bt_h, lt_h, ls_h, ut_h, us_h, lsrc, lc_h, nb_h, nt_v, nsrc, ncnt,
    out_h,
    em, bs, bt, lt, ls, ut, us, lc, nb,
    eh, halo, gath, dup, mp, mb, mu, eu, su, lev, sib, ylev, carried,
    xr, zr, upair, prod, nacc, cp, out,
    load_sem, nb_sem, lc_sem, bs_sem, out_sem, halo_s, halo_r,
    own_s, fwd_s, gath_r, xr_s, xr_r, zr_s, zr_r,
):
    row, col = lax.axis_index("row"), lax.axis_index("col")
    device = row * COLS + col
    z, core = col // 2, col % 2
    sibling = z * 2 + 1 - core
    znext = lax.rem(z + 1, 4)
    zprev = lax.rem(z + 3, 4)
    zfar = lax.rem(z + 2, 4)
    up_col, down_col, far_col = znext * 2 + core, zprev * 2 + core, zfar * 2 + core

    def load(src, dst, i):
        c = pltpu.make_async_copy(src, dst, load_sem.at[i])
        c.start()
        return c

    em_c = load(em_h, em, 0)
    width = 8192 // CHUNKS
    bs_c = []
    for k in range(CHUNKS):
        c = pltpu.make_async_copy(
            bs_h.at[:, pl.ds(k * width, width)], bs.at[:, pl.ds(k * width, width)], bs_sem.at[k]
        )
        c.start()
        bs_c.append(c)

    barrier = pltpu.get_barrier_semaphore()
    nxt, prv = lax.rem(device + 1, ROWS * COLS), lax.rem(device + ROWS * COLS - 1, ROWS * COLS)
    next_id = (nxt // COLS, lax.rem(nxt, COLS))
    prev_id = (prv // COLS, lax.rem(prv, COLS))
    for i in range(1, COLS):
        pl.semaphore_signal(barrier, 1, device_id=(row, lax.rem(col + i, COLS)), device_id_type=MESH)
    for i in range(1, ROWS):
        pl.semaphore_signal(barrier, 1, device_id=(lax.rem(row + i, ROWS), col), device_id_type=MESH)
    pl.semaphore_signal(barrier, 1, device_id=next_id, device_id_type=MESH)
    pl.semaphore_signal(barrier, 1, device_id=prev_id, device_id_type=MESH)

    per, lper = SLOTS // NEAR_PARTS, LEAVES // NEAR_PARTS

    def load_near(k):
        pltpu.make_async_copy(
            nb_h.at[pl.ds(k * per, per)], nb.at[pl.ds(k * per, per)], nb_sem.at[k]).start()
        pltpu.make_async_copy(
            lc_h.at[pl.ds(k * lper, lper)], lc.at[pl.ds(k * lper, lper)], lc_sem.at[k]).start()

    lane = lax.broadcasted_iota(jnp.int32, (RHS, 128), 1)
    first_half = lane < 64
    lane2 = lax.broadcasted_iota(jnp.int32, (2 * RHS, 128), 1)
    first_half2 = lane2 < 64

    em_c.wait()
    lt_c = load(lt_h, lt, 1)

    def split_leaf(g, carry):
        for u in range(8):
            l = g * 8 + u
            eh[l + 1] = split(em[:, pl.ds(pl.multiple_of(l * LEAF, LEAF), LEAF)])
        return carry

    lax.fori_loop(0, LEAVES // 8, split_leaf, 0)

    pl.semaphore_wait(barrier, COLS - 1 + ROWS - 1 + 2)

    halo_next = pltpu.make_async_remote_copy(
        em.at[:, pl.ds((LEAVES - 1) * LEAF, LEAF)], halo.at[0], halo_s.at[0], halo_r.at[0],
        device_id=next_id, device_id_type=MESH)
    halo_prev = pltpu.make_async_remote_copy(
        em.at[:, pl.ds(0, LEAF)], halo.at[1], halo_s.at[1], halo_r.at[1],
        device_id=prev_id, device_id_type=MESH)
    halo_next.start()
    halo_prev.start()

    def piece(owner, k):
        return gath.at[owner, pl.ds(k * PART, PART)]

    def send(owner, k, to_col, send_sem, kind):
        return pltpu.make_async_remote_copy(
            piece(owner, k), piece(owner, k), send_sem, gath_r.at[kind, k],
            device_id=(row, to_col), device_id_type=MESH)

    sends = []

    def leaf_pair(p):
        a = eh[pl.ds(2 * p + 1, 2)].reshape(64, 128)
        start = pl.multiple_of(p * 256, 256)
        w = bs[:, pl.ds(start, 256)]
        b = jnp.concatenate([w[:, :128], w[:, 128:]], axis=0)
        o = dot_nt(a, b)
        gath[col, p] = jnp.where(first_half, o[0:16] + o[16:32], o[32:48] + o[48:64])

    for k in range(CHUNKS):
        bs_c[k].wait()

        def leaf_step(g, carry, k=k):
            for u in range(8):
                leaf_pair(k * PART + g * 8 + u)
            return carry

        lax.fori_loop(0, PART // 8, leaf_step, 0)
        for n, (to_col, kind) in enumerate(((up_col, 1), (down_col, 2), (sibling, 0))):
            c = send(col, k, to_col, own_s.at[n, k], kind)
            c.start()
            sends.append(c)

    def recv(owner, k, kind):
        pltpu.make_async_remote_copy(
            piece(owner, k), piece(owner, k), own_s.at[0, k], gath_r.at[kind, k],
            device_id=(row, col), device_id_type=MESH).wait_recv()

    def relay_near(k):
        recv(down_col, k, 1)
        if k < CHUNKS // 2:
            c = send(down_col, k, up_col, fwd_s.at[0, k], 3)
            c.start()
            sends.append(c)
        c = send(down_col, k, sibling, fwd_s.at[1, k], 4)
        c.start()
        sends.append(c)
        recv(up_col, k, 2)
        if k >= CHUNKS // 2:
            c = send(up_col, k, down_col, fwd_s.at[0, k], 3)
            c.start()
            sends.append(c)
        c = send(up_col, k, sibling, fwd_s.at[2, k], 5)
        c.start()
        sends.append(c)

    def relay_far(k):
        recv(far_col, k, 3)
        c = send(far_col, k, sibling, fwd_s.at[3, k], 6)
        c.start()
        sends.append(c)

    ut_c = load(ut_h, ut, 2)
    us_c = load(us_h, us, 3)
    lt_c.wait()
    load_near(0)
    ls_c = load(ls_h, ls, 4)
    for k in range(1, NEAR_PARTS):
        load_near(k)
    bt_c = load(bt_h, bt, 5)
    eye = (
        lax.broadcasted_iota(jnp.int32, (128, 126), 0)
        == lax.broadcasted_iota(jnp.int32, (128, 126), 1)
    ).astype(BF16)

    def turn_local(q, carry):
        w = jnp.concatenate([lt[q], lt[q + 32]], axis=0)
        mp[pl.ds(q, 128, stride=MAT), :] = dot_nt(eye, w)
        return carry

    lax.fori_loop(0, 32, turn_local, 0, unroll=4)

    def unpack(source, target, n):
        m = source[pl.ds(n * MAT, 32), :].astype(BF16)
        target[n] = jnp.concatenate([m[:, :64], m[:, 64:]], axis=0)

    def unpack_local(g, carry):
        for u in range(18):
            unpack(mp, mb, g * 18 + u)
        return carry

    lax.fori_loop(0, 7, unpack_local, 0)

    relay_near(0)

    def lift(pair, weights):
        return joined(dot_nn(split(pair), weights.reshape(128, 64)))

    def level_pair(h, p):
        return gath[col, p] if h == 0 else lev[lev_base(h) + p]

    for h in range(HEIGHT - 1):
        count = PAIRS >> h
        off = level_offset(h)

        def up_two(q, h=h, off=off):
            one = lift(level_pair(h, 2 * q), mb[pl.ds(off + 4 * q, 2)])
            two = lift(level_pair(h, 2 * q + 1), mb[pl.ds(off + 4 * q + 2, 2)])
            lev[lev_base(h + 1) + q] = jnp.concatenate([one, two], axis=1)

        half = count // 2
        group = min(half, 8)

        def up_step(g, carry, up_two=up_two, group=group):
            for u in range(group):
                up_two(g * group + u)
            return carry

        lax.fori_loop(0, half // group, up_step, 0)
    root = lift(lev[lev_base(5)], mb[pl.ds(level_offset(5), 2)])

    def placed(value, parity):
        return jnp.where(
            (lane >= 64).astype(jnp.int32) == parity, jnp.concatenate([value, value], axis=1), 0.0
        )

    xr[col] = placed(root, core)
    xr_copies = []
    for i in range(1, COLS):
        c = pltpu.make_async_remote_copy(
            xr.at[col], xr.at[col], xr_s.at[i], xr_r.at[i],
            device_id=(row, lax.rem(col + i, COLS)), device_id_type=MESH)
        c.start()
        xr_copies.append(c)

    relay_near(1)

    ut_c.wait()
    us_c.wait()
    picks = lax.broadcasted_iota(jnp.int32, (64, 254), 0)
    cluster = lax.broadcasted_iota(jnp.int32, (64, 254), 1)
    want = jnp.where(picks < 8, row * 8 + picks, -1)
    want = jnp.where((picks >= 8) & (picks < 12), 128 + row * 4 + picks - 8, want)
    want = jnp.where((picks >= 12) & (picks < 14), 192 + row * 2 + picks - 12, want)
    want = jnp.where((picks >= 16) & (picks < 46), 224 + picks - 16, want)
    for j in range(7):
        want = jnp.where(picks == 48 + j, 256 - (256 >> j) + (device // (1 << j)), want)
    pick_u = (cluster == want).astype(BF16)
    picks_s = lax.broadcasted_iota(jnp.int32, (16, 254), 0)
    cluster_s = lax.broadcasted_iota(jnp.int32, (16, 254), 1)
    want_s = jnp.full((16, 254), -1, jnp.int32)
    for j in range(7):
        want_s = jnp.where(picks_s == j, 256 - (256 >> j) + (device // (1 << j)), want_s)
    pick_s = (cluster_s == want_s).astype(BF16)

    def turn_upper(q, carry):
        w = jnp.concatenate([ut[q], ut[q + 32]], axis=0)
        mu[pl.ds(q, 64, stride=MAT), :] = dot_nt(pick_u, w)
        w = jnp.concatenate([us[q], us[q + 32]], axis=0)
        mp[pl.ds(q, 16, stride=MAT), :] = dot_nt(pick_s, w)
        return carry

    lax.fori_loop(0, 32, turn_upper, 0, unroll=4)

    def unpack_upper(g, carry):
        for u in range(16):
            unpack(mu, eu, g * 16 + u)
        for u in range(2):
            unpack(mp, su, g * 2 + u)
        return carry

    lax.fori_loop(0, 4, unpack_upper, 0)

    relay_near(2)

    for i in range(1, COLS):
        peer = lax.rem(col + COLS - i, COLS)
        pltpu.make_async_remote_copy(
            xr.at[peer], xr.at[peer], xr_s.at[i], xr_r.at[i],
            device_id=(row, peer), device_id_type=MESH).wait_recv()
    for i in range(4):
        upair[i] = xr[2 * i] + xr[2 * i + 1]

    def up_upper(source, count, target, first):
        for i in range(count // 2):
            one = lift(upair[source + 2 * i], eu[first + 4 * i : first + 4 * i + 2])
            two = lift(upair[source + 2 * i + 1], eu[first + 4 * i + 2 : first + 4 * i + 4])
            upair[target + i] = jnp.concatenate([one, two], axis=1)

    up_upper(0, 4, 4, 0)
    up_upper(4, 2, 6, 8)
    row_root = lift(upair[6], eu[12:14])
    zr[row] = placed(row_root, lax.rem(row, 2))
    zr_copies = []
    for i in range(1, ROWS):
        c = pltpu.make_async_remote_copy(
            zr.at[row], zr.at[row], zr_s.at[i], zr_r.at[i],
            device_id=(lax.rem(row + i, ROWS), col), device_id_type=MESH)
        c.start()
        zr_copies.append(c)

    relay_near(3)

    halo_next.wait_recv()
    halo_prev.wait_recv()
    eh[0] = split(halo[0])
    eh[LEAVES + 1] = split(halo[1])
    leaf_first = device * LEAVES
    zero = jnp.zeros((2 * RHS, LEAF), BF16)

    def near_part(k):
        pltpu.make_async_copy(
            nb_h.at[pl.ds(k * per, per)], nb.at[pl.ds(k * per, per)], nb_sem.at[k]).wait()
        pltpu.make_async_copy(
            lc_h.at[pl.ds(k * lper, lper)], lc.at[pl.ds(k * lper, lper)], lc_sem.at[k]).wait()

        def near_step(g, carry):
            for u in range(12):
                s = k * per + g * 24 + 2 * u
                one, two = (
                    eh[jnp.clip(nsrc[s + i] - leaf_first + 1, 0, LEAVES + 1)] for i in range(2))
                lhs = jnp.concatenate(
                    [jnp.concatenate([one, zero], axis=1), jnp.concatenate([zero, two], axis=1)],
                    axis=0)
                o = dot_nt(lhs, jnp.concatenate([nb[s], nb[s + 1]], axis=1))
                prod[pl.ds(s, RHS, stride=SLOT_ROWS), :] = joined(o[:32])
                prod[pl.ds(s + 1, RHS, stride=SLOT_ROWS), :] = joined(o[32:])
                if u < 8:
                    t = k * lper + g * 8 + u
                    cp[t] = jnp.concatenate([lc[t, 0], lc[t, 1], lc[t, 2], lc[t, 3]], axis=1)
            return carry

        lax.fori_loop(0, per // 24, near_step, 0)

    near_part(0)
    relay_far(0)
    relay_far(1)
    near_part(1)
    relay_far(2)
    near_part(2)

    ls_c.wait()
    for h in range(1, HEIGHT):
        count = PAIRS >> h

        def sib_one(p, h=h):
            x = lev[lev_base(h) + p]
            lhs = jnp.concatenate([split(x[:, 64:]), split(x[:, :64])], axis=0)
            w = ls[pl.ds(LEAVES - 2 * (LEAVES >> h) + 2 * p, 2)].reshape(128, 64)
            o = dot_nt(lhs, w)
            sib[lev_base(h) + p] = jnp.where(first_half, o[0:16] + o[16:32], o[32:48] + o[48:64])

        group = min(count, 8)

        def sib_step(g, carry, sib_one=sib_one, group=group):
            for u in range(group):
                sib_one(g * group + u)
            return carry

        lax.fori_loop(0, count // group, sib_step, 0)

    relay_far(3)
    near_part(3)

    for i in range(1, ROWS):
        peer = lax.rem(row + ROWS - i, ROWS)
        pltpu.make_async_remote_copy(
            zr.at[peer], zr.at[peer], zr_s.at[i], zr_r.at[i],
            device_id=(peer, col), device_id_type=MESH).wait_recv()
    for i in range(8):
        upair[7 + i] = zr[2 * i] + zr[2 * i + 1]
    up_upper(7, 8, 15, 16)
    up_upper(15, 4, 19, 32)
    up_upper(19, 2, 21, 40)

    own = []
    for j, base in enumerate((0, 4, 6, 7, 15, 19, 21)):
        own.append((base, col // (1 << j)) if j < 3 else (base, row // (1 << (j - 3))))
    y = jnp.zeros((RHS, RANK), F32)
    for j in range(6, -1, -1):
        base, mine = own[j]
        pair = upair[base + mine // 2]
        turned = jnp.concatenate([pair[:, 64:], pair[:, :64]], axis=1)
        other = jnp.where(lax.rem(mine, 2) == 1, pair, turned)[:, :64]
        y = joined(dot_nt(split(other), su[j])) + joined(dot_nt(split(y), eu[48 + j]))

    ylev[30] = placed(y, 0)
    for h in range(HEIGHT - 1, -1, -1):
        count = PAIRS >> h
        off = level_offset(h)

        def down_one(parent, p, h=h, off=off):
            w = mb[pl.ds(off + 2 * p, 2)].reshape(128, 64)
            value = joined(dot_nt(split(parent), w))
            if h:
                ylev[lev_base(h) + p] = value + sib[lev_base(h) + p]
            else:
                carried[p] = value

        if h == HEIGHT - 1:
            down_one(y, 0)
            continue

        def down_two(q, h=h, down_one=down_one):
            pair = ylev[lev_base(h + 1) + q]
            down_one(pair[:, :64], 2 * q)
            down_one(pair[:, 64:], 2 * q + 1)

        half = count // 2
        group = min(half, 8)

        def down_step(g, carry, down_two=down_two, group=group):
            for u in range(group):
                down_two(g * group + u)
            return carry

        lax.fori_loop(0, half // group, down_step, 0)

    target = nt_v[...] - leaf_first
    slot = lax.broadcasted_iota(jnp.int32, (LEAVES, SLOTS), 1)
    one_hot = (
        (jnp.broadcast_to(target, (LEAVES, SLOTS))
         == lax.broadcasted_iota(jnp.int32, (LEAVES, SLOTS), 0))
        & (slot < ncnt[0])
    ).astype(BF16)

    def sum_step(g, carry):
        for u in range(4):
            r = g * 4 + u
            x = prod[pl.ds(r * SLOT_ROWS, SLOTS), :]
            high = x.astype(BF16)
            low = (x - high.astype(F32)).astype(BF16)
            nacc[pl.ds(r, LEAVES, stride=LEAF_ROWS), :] = dot_nn(one_hot, high) + dot_nn(one_hot, low)
        return carry

    lax.fori_loop(0, RHS // 4, sum_step, 0)

    def dup_part(owner, k):
        def dup_step(g, carry):
            for u in range(8):
                p = k * PART + g * 8 + u
                x = gath[owner, p]
                turned = jnp.concatenate([x[:, 64:], x[:, :64]], axis=1)
                base = owner * LEAVES + 2 * p
                dup[base] = split(jnp.where(first_half, x, turned))
                dup[base + 1] = split(jnp.where(first_half, turned, x))
            return carry

        lax.fori_loop(0, PART // 8, dup_step, 0)

    other = 1 - core
    for k in range(CHUNKS):
        dup_part(col, k)
        dup_part(down_col, k)
        dup_part(up_col, k)
        recv(sibling, k, 0)
        dup_part(sibling, k)
        recv(zprev * 2 + other, k, 4)
        dup_part(zprev * 2 + other, k)
        recv(znext * 2 + other, k, 5)
        dup_part(znext * 2 + other, k)
    for k in range(CHUNKS):
        dup_part(far_col, k)
        recv(zfar * 2 + other, k, 6)
        dup_part(zfar * 2 + other, k)

    bt_c.wait()
    group_first = row * (LEAVES * COLS)

    def final_step(g, carry):
        pairs = [g * (FINAL // 2) + u for u in range(FINAL // 2)]

        def listed_of(t):
            d = [dup[jnp.clip(lsrc[j, t] - group_first, 0, LEAVES * COLS - 1)]
                 for j in range(PARTNERS)]
            return jnp.concatenate(
                [jnp.where(first_half2, d[0], d[1]), jnp.where(first_half2, d[2], d[3])], axis=1)

        lhs = [jnp.concatenate([listed_of(2 * q), listed_of(2 * q + 1)], axis=0) for q in pairs]
        listed = [dot_nt(x, cp[pl.ds(2 * q, 2)].reshape(128, 256)) for x, q in zip(lhs, pairs)]
        y0 = []
        for o, q in zip(listed, pairs):
            c = carried[q]
            one = jnp.where(first_half, joined(o[:32]) + c, 0.0)
            two = jnp.where(first_half, 0.0, joined(o[32:]) + c)
            y0.append(jnp.concatenate([split(one), split(two)], axis=0))
        starts = [pl.multiple_of(q * 2 * LEAF, 2 * LEAF) for q in pairs]
        far = []
        for y, start in zip(y0, starts):
            w = bt[:, pl.ds(start, 2 * LEAF)]
            far.append(dot_nn(y, jnp.concatenate([w[:, :LEAF], w[:, LEAF:]], axis=0)))
        for o, q, start in zip(far, pairs, starts):
            out[:, pl.ds(start, 2 * LEAF)] = jnp.concatenate(
                [joined(o[:32]) + nacc[pl.ds(2 * q * LEAF_ROWS, RHS), :],
                 joined(o[32:]) + nacc[pl.ds((2 * q + 1) * LEAF_ROWS, RHS), :]], axis=1)
        return carry

    lax.fori_loop(0, LEAVES // FINAL, final_step, 0)
    out_c = pltpu.make_async_copy(out, out_h, out_sem)
    out_c.start()
    halo_next.wait_send()
    halo_prev.wait_send()
    for c in sends + xr_copies + zr_copies:
        c.wait_send()
    out_c.wait()


def shards(
    emission, basis_source, basis_target, local_transfer, local_sibling, upper_transfer,
    upper_sibling, leaf_source, leaf_coupling, near_block, near_target, near_source, near_count,
):
    hbm = pl.BlockSpec(memory_space=pl.ANY)
    smem = pl.BlockSpec(memory_space=pltpu.SMEM)
    vmem = pl.BlockSpec(memory_space=pltpu.VMEM)
    dma = pltpu.SemaphoreType.DMA
    V = pltpu.VMEM
    return pl.pallas_call(
        kernel,
        out_shape=jax.ShapeDtypeStruct((RHS, LEAVES * LEAF), F32),
        in_specs=[hbm] * 7 + [smem, hbm, hbm, vmem, smem, smem],
        out_specs=hbm,
        scratch_shapes=[
            V((RHS, 8192), F32), V((RANK, 8192), BF16), V((RANK, 8192), BF16),
            V((64, 64, 126), BF16), V((62, 64, 64), BF16),
            V((64, 64, 254), BF16), V((64, 64, 254), BF16),
            V((LEAVES, PARTNERS, 64, 64), BF16), V((SLOTS, 128, 128), BF16),
            V((LEAVES + 2, 32, 128), BF16),
            V((2, RHS, 128), F32),
            V((COLS, PAIRS, RHS, 128), F32),
            V((COLS * LEAVES, 32, 128), BF16),
            V((128 * MAT, 128), F32),
            V((126, 64, 64), BF16),
            V((64 * MAT, 128), F32),
            V((64, 64, 64), BF16),
            V((8, 64, 64), BF16),
            V((32, RHS, 128), F32),
            V((32, RHS, 128), F32),
            V((32, RHS, 128), F32),
            V((PAIRS, RHS, 128), F32),
            V((COLS, RHS, 128), F32),
            V((ROWS, RHS, 128), F32),
            V((22, RHS, 128), F32),
            V((RHS * SLOT_ROWS, 128), F32),
            V((LEAVES * LEAF_ROWS, 128), F32),
            V((LEAVES, 64, 256), BF16),
            V((RHS, 8192), F32),
            dma((6,)), dma((NEAR_PARTS,)), dma((NEAR_PARTS,)), dma((CHUNKS,)), dma, dma((2,)), dma((2,)),
            dma((3, CHUNKS)), dma((4, CHUNKS)), dma((7, CHUNKS)),
            dma((COLS,)), dma((COLS,)), dma((ROWS,)), dma((ROWS,)),
        ],
        compiler_params=pltpu.CompilerParams(
            collective_id=0, has_side_effects=True, vmem_limit_bytes=58 * 1024 * 1024),
        name="h2_product",
    )(
        emission, basis_source, basis_target, local_transfer.transpose(1, 2, 0), local_sibling,
        upper_transfer.transpose(1, 2, 0), upper_sibling.transpose(1, 2, 0), leaf_source.T,
        leaf_coupling, near_block, near_target.reshape(1, SLOTS), near_source, near_count,
    )


def solution(mesh):
    both = ("row", "col")
    in_specs = (
        P(None, both), P(None, both), P(None, both), P(both, None, None), P(both, None, None),
        P(), P(), P(both, None), P(both, None, None, None), P(both, None, None),
        P(both), P(both), P(both),
    )
    return jax.shard_map(
        shards, mesh=mesh, in_specs=in_specs, out_specs=P(None, both), check_vma=False)
```

```python
import functools

import jax
import jax.numpy as jnp
from jax import lax
from jax.experimental import pallas as pl
from jax.experimental.pallas import tpu as pltpu
from jax.sharding import PartitionSpec as P

MESH = pl.DeviceIdType.MESH
F32 = jnp.float32
BF16 = jnp.bfloat16

RHS = 16
RANK = 64
LEAF = 128
LEAVES = 64
PAIRS = LEAVES // 2
PARTNERS = 4
SLOTS = 192
ROWS, COLS = 16, 8
CHUNKS = 2
PART = PAIRS // CHUNKS
HEIGHT = 6
NEAR_PARTS = 4
FINAL = 16
MAT, SLOT_ROWS, LEAF_ROWS = 33, SLOTS + 1, RHS + 1


def dot_nn(a, b):
    return lax.dot_general(a, b, (((1,), (0,)), ((), ())), preferred_element_type=F32)


def dot_nt(a, b):
    return lax.dot_general(a, b, (((1,), (1,)), ((), ())), preferred_element_type=F32)


def split(x):
    high = x.astype(BF16)
    low = (x - high.astype(F32)).astype(BF16)
    return jnp.concatenate([high, low], axis=0)


def joined(o):
    half = o.shape[0] // 2
    return o[:half] + o[half:]


def level_offset(h):
    return 2 * LEAVES - 2 * (LEAVES >> h)


def lev_base(h):
    return PAIRS - (PAIRS >> (h - 1)) if h >= 1 else 0


def kernel(
    em_h, bs_h, bt_h, lt_h, ls_h, ut_h, us_h, lsrc, lc_h, nb_h, nt_v, nsrc, ncnt,
    out,
    em, bs, bt, lt, ls, ut, us, lc, nb,
    eh, halo, gath, dup, mp, mb, mu, eu, su, lev, sib, ylev, carried,
    xr, zr, upair, prod, nacc, cp,
    load_sem, nb_sem, lc_sem, bs_sem, halo_s, halo_r,
    own_s, fwd_s, gath_r, xr_s, xr_r, zr_s, zr_r,
):
    row, col = lax.axis_index("row"), lax.axis_index("col")
    device = row * COLS + col
    z, core = col // 2, col % 2
    sibling = z * 2 + 1 - core
    znext = lax.rem(z + 1, 4)
    zprev = lax.rem(z + 3, 4)
    zfar = lax.rem(z + 2, 4)
    up_col, down_col, far_col = znext * 2 + core, zprev * 2 + core, zfar * 2 + core

    def load(src, dst, i):
        c = pltpu.make_async_copy(src, dst, load_sem.at[i])
        c.start()
        return c

    em_c = load(em_h, em, 0)
    width = 8192 // CHUNKS
    bs_c = []
    for k in range(CHUNKS):
        c = pltpu.make_async_copy(
            bs_h.at[:, pl.ds(k * width, width)], bs.at[:, pl.ds(k * width, width)], bs_sem.at[k]
        )
        c.start()
        bs_c.append(c)

    barrier = pltpu.get_barrier_semaphore()
    nxt, prv = lax.rem(device + 1, ROWS * COLS), lax.rem(device + ROWS * COLS - 1, ROWS * COLS)
    next_id = (nxt // COLS, lax.rem(nxt, COLS))
    prev_id = (prv // COLS, lax.rem(prv, COLS))
    for i in range(1, COLS):
        pl.semaphore_signal(barrier, 1, device_id=(row, lax.rem(col + i, COLS)), device_id_type=MESH)
    for i in range(1, ROWS):
        pl.semaphore_signal(barrier, 1, device_id=(lax.rem(row + i, ROWS), col), device_id_type=MESH)
    pl.semaphore_signal(barrier, 1, device_id=next_id, device_id_type=MESH)
    pl.semaphore_signal(barrier, 1, device_id=prev_id, device_id_type=MESH)

    per, lper = SLOTS // NEAR_PARTS, LEAVES // NEAR_PARTS

    def load_near(k):
        pltpu.make_async_copy(
            nb_h.at[pl.ds(k * per, per)], nb.at[pl.ds(k * per, per)], nb_sem.at[k]).start()
        pltpu.make_async_copy(
            lc_h.at[pl.ds(k * lper, lper)], lc.at[pl.ds(k * lper, lper)], lc_sem.at[k]).start()

    lane = lax.broadcasted_iota(jnp.int32, (RHS, 128), 1)
    first_half = lane < 64
    lane2 = lax.broadcasted_iota(jnp.int32, (2 * RHS, 128), 1)
    first_half2 = lane2 < 64

    em_c.wait()
    lt_c = load(lt_h, lt, 1)

    def split_leaf(g, carry):
        for u in range(8):
            l = g * 8 + u
            eh[l + 1] = split(em[:, pl.ds(pl.multiple_of(l * LEAF, LEAF), LEAF)])
        return carry

    lax.fori_loop(0, LEAVES // 8, split_leaf, 0)

    def piece(owner, k):
        return gath.at[owner, pl.ds(k * PART, PART)]

    def send(owner, k, to_col, send_sem, kind):
        return pltpu.make_async_remote_copy(
            piece(owner, k), piece(owner, k), send_sem, gath_r.at[kind, k],
            device_id=(row, to_col), device_id_type=MESH)

    sends = []

    def begin(owner, k, to_col, send_sem, kind):
        c = send(owner, k, to_col, send_sem, kind)
        c.start()
        sends.append(c)

    def leaf_pair(p):
        a = eh[pl.ds(2 * p + 1, 2)].reshape(64, 128)
        start = pl.multiple_of(p * 256, 256)
        w = bs[:, pl.ds(start, 256)]
        b = jnp.concatenate([w[:, :128], w[:, 128:]], axis=0)
        o = dot_nt(a, b)
        gath[col, p] = jnp.where(first_half, o[0:16] + o[16:32], o[32:48] + o[48:64])

    for k in range(CHUNKS):
        bs_c[k].wait()

        def leaf_step(g, carry, k=k):
            for u in range(8):
                leaf_pair(k * PART + g * 8 + u)
            return carry

        lax.fori_loop(0, PART // 8, leaf_step, 0)

    def recv(owner, k, kind):
        pltpu.make_async_remote_copy(
            piece(owner, k), piece(owner, k), own_s.at[0, k], gath_r.at[kind, k],
            device_id=(row, col), device_id_type=MESH).wait_recv()

    def relay_first():
        recv(down_col, 0, 1)
        begin(down_col, 0, up_col, fwd_s.at[0, 0], 3)
        recv(up_col, 1, 2)
        begin(up_col, 1, down_col, fwd_s.at[0, 1], 3)
        begin(down_col, 0, sibling, fwd_s.at[1, 0], 4)
        begin(up_col, 1, sibling, fwd_s.at[2, 1], 5)

    def relay_second():
        recv(down_col, 1, 1)
        begin(down_col, 1, sibling, fwd_s.at[1, 1], 4)
        recv(up_col, 0, 2)
        begin(up_col, 0, sibling, fwd_s.at[2, 0], 5)

    def relay_far():
        for k in range(CHUNKS):
            recv(far_col, k, 3)
            begin(far_col, k, sibling, fwd_s.at[3, k], 6)

    ut_c = load(ut_h, ut, 2)
    us_c = load(us_h, us, 3)
    lt_c.wait()
    load_near(0)
    ls_c = load(ls_h, ls, 4)
    for k in range(1, NEAR_PARTS):
        load_near(k)
    bt_c = load(bt_h, bt, 5)
    eye = (
        lax.broadcasted_iota(jnp.int32, (128, 126), 0)
        == lax.broadcasted_iota(jnp.int32, (128, 126), 1)
    ).astype(BF16)

    def turn_local(q, carry):
        w = jnp.concatenate([lt[q], lt[q + 32]], axis=0)
        mp[pl.ds(q, 128, stride=MAT), :] = dot_nt(eye, w)
        return carry

    lax.fori_loop(0, 32, turn_local, 0, unroll=4)

    def unpack(source, target, n):
        m = source[pl.ds(n * MAT, 32), :].astype(BF16)
        target[n] = jnp.concatenate([m[:, :64], m[:, 64:]], axis=0)

    def unpack_local(g, carry):
        for u in range(18):
            unpack(mp, mb, g * 18 + u)
        return carry

    lax.fori_loop(0, 7, unpack_local, 0)

    def lift(pair, weights):
        return joined(dot_nn(split(pair), weights.reshape(128, 64)))

    zero = jnp.zeros((2 * RHS, LEAF), BF16)

    def lift_two(one, two, weights):
        lhs = jnp.concatenate(
            [jnp.concatenate([split(one), zero], axis=1),
             jnp.concatenate([zero, split(two)], axis=1)], axis=0)
        o = dot_nn(lhs, weights.reshape(256, 64))
        return jnp.concatenate([joined(o[:32]), joined(o[32:])], axis=1)

    def level_pair(h, p):
        return gath[col, p] if h == 0 else lev[lev_base(h) + p]

    for h in range(HEIGHT - 1):
        count = PAIRS >> h
        off = level_offset(h)

        def up_two(q, h=h, off=off):
            lev[lev_base(h + 1) + q] = lift_two(
                level_pair(h, 2 * q), level_pair(h, 2 * q + 1), mb[pl.ds(off + 4 * q, 4)])

        half = count // 2
        group = min(half, 8)

        def up_step(g, carry, up_two=up_two, group=group):
            for u in range(group):
                up_two(g * group + u)
            return carry

        lax.fori_loop(0, half // group, up_step, 0)
    root = lift(lev[lev_base(5)], mb[pl.ds(level_offset(5), 2)])

    def placed(value, parity):
        return jnp.where(
            (lane >= 64).astype(jnp.int32) == parity, jnp.concatenate([value, value], axis=1), 0.0
        )

    xr[col] = placed(root, core)
    pl.semaphore_wait(barrier, COLS - 1 + ROWS - 1 + 2)

    halo_next = pltpu.make_async_remote_copy(
        em.at[:, pl.ds((LEAVES - 1) * LEAF, LEAF)], halo.at[0], halo_s.at[0], halo_r.at[0],
        device_id=next_id, device_id_type=MESH)
    halo_prev = pltpu.make_async_remote_copy(
        em.at[:, pl.ds(0, LEAF)], halo.at[1], halo_s.at[1], halo_r.at[1],
        device_id=prev_id, device_id_type=MESH)
    halo_next.start()
    halo_prev.start()

    xr_copies = []
    for i in range(1, COLS):
        c = pltpu.make_async_remote_copy(
            xr.at[col], xr.at[col], xr_s.at[i], xr_r.at[i],
            device_id=(row, lax.rem(col + i, COLS)), device_id_type=MESH)
        c.start()
        xr_copies.append(c)

    begin(col, 0, up_col, own_s.at[0, 0], 1)
    begin(col, 1, down_col, own_s.at[1, 1], 2)
    for k in range(CHUNKS):
        begin(col, k, sibling, own_s.at[2, k], 0)
    begin(col, 1, up_col, own_s.at[0, 1], 1)
    begin(col, 0, down_col, own_s.at[1, 0], 2)

    ut_c.wait()
    us_c.wait()
    picks = lax.broadcasted_iota(jnp.int32, (64, 254), 0)
    cluster = lax.broadcasted_iota(jnp.int32, (64, 254), 1)
    want = jnp.where(picks < 8, row * 8 + picks, -1)
    want = jnp.where((picks >= 8) & (picks < 12), 128 + row * 4 + picks - 8, want)
    want = jnp.where((picks >= 12) & (picks < 14), 192 + row * 2 + picks - 12, want)
    want = jnp.where((picks >= 16) & (picks < 46), 224 + picks - 16, want)
    for j in range(7):
        want = jnp.where(picks == 48 + j, 256 - (256 >> j) + (device // (1 << j)), want)
    pick_u = (cluster == want).astype(BF16)
    picks_s = lax.broadcasted_iota(jnp.int32, (16, 254), 0)
    cluster_s = lax.broadcasted_iota(jnp.int32, (16, 254), 1)
    want_s = jnp.full((16, 254), -1, jnp.int32)
    for j in range(7):
        want_s = jnp.where(picks_s == j, 256 - (256 >> j) + (device // (1 << j)), want_s)
    pick_s = (cluster_s == want_s).astype(BF16)

    def turn_upper(q, carry):
        w = jnp.concatenate([ut[q], ut[q + 32]], axis=0)
        mu[pl.ds(q, 64, stride=MAT), :] = dot_nt(pick_u, w)
        w = jnp.concatenate([us[q], us[q + 32]], axis=0)
        mp[pl.ds(q, 16, stride=MAT), :] = dot_nt(pick_s, w)
        return carry

    lax.fori_loop(0, 32, turn_upper, 0, unroll=4)

    def unpack_upper(g, carry):
        for u in range(16):
            unpack(mu, eu, g * 16 + u)
        for u in range(2):
            unpack(mp, su, g * 2 + u)
        return carry

    lax.fori_loop(0, 4, unpack_upper, 0)

    halo_next.wait_recv()
    halo_prev.wait_recv()
    eh[0] = split(halo[0])
    eh[LEAVES + 1] = split(halo[1])
    leaf_first = device * LEAVES
    def near_part(k):
        pltpu.make_async_copy(
            nb_h.at[pl.ds(k * per, per)], nb.at[pl.ds(k * per, per)], nb_sem.at[k]).wait()
        pltpu.make_async_copy(
            lc_h.at[pl.ds(k * lper, lper)], lc.at[pl.ds(k * lper, lper)], lc_sem.at[k]).wait()

        def near_step(g, carry):
            for u in range(12):
                s = k * per + g * 24 + 2 * u
                one, two = (
                    eh[jnp.clip(nsrc[s + i] - leaf_first + 1, 0, LEAVES + 1)] for i in range(2))
                lhs = jnp.concatenate(
                    [jnp.concatenate([one, zero], axis=1), jnp.concatenate([zero, two], axis=1)],
                    axis=0)
                o = dot_nt(lhs, jnp.concatenate([nb[s], nb[s + 1]], axis=1))
                prod[pl.ds(s, RHS, stride=SLOT_ROWS), :] = joined(o[:32])
                prod[pl.ds(s + 1, RHS, stride=SLOT_ROWS), :] = joined(o[32:])
                if u < 8:
                    t = k * lper + g * 8 + u
                    cp[t] = jnp.concatenate([lc[t, 0], lc[t, 1], lc[t, 2], lc[t, 3]], axis=1)
            return carry

        lax.fori_loop(0, per // 24, near_step, 0)

    near_part(0)

    for i in range(1, COLS):
        peer = lax.rem(col + COLS - i, COLS)
        pltpu.make_async_remote_copy(
            xr.at[peer], xr.at[peer], xr_s.at[i], xr_r.at[i],
            device_id=(row, peer), device_id_type=MESH).wait_recv()
    for i in range(4):
        upair[i] = xr[2 * i] + xr[2 * i + 1]

    def up_upper(source, count, target, first):
        for i in range(count // 2):
            upair[target + i] = lift_two(
                upair[source + 2 * i], upair[source + 2 * i + 1],
                eu[first + 4 * i : first + 4 * i + 4])

    up_upper(0, 4, 4, 0)
    up_upper(4, 2, 6, 8)
    row_root = lift(upair[6], eu[12:14])
    zr[row] = placed(row_root, lax.rem(row, 2))
    zr_copies = []
    for i in range(1, ROWS):
        c = pltpu.make_async_remote_copy(
            zr.at[row], zr.at[row], zr_s.at[i], zr_r.at[i],
            device_id=(lax.rem(row + i, ROWS), col), device_id_type=MESH)
        c.start()
        zr_copies.append(c)

    near_part(1)
    near_part(2)
    relay_first()
    near_part(3)

    ls_c.wait()
    for h in range(1, HEIGHT):
        count = PAIRS >> h

        def sib_one(p, h=h):
            x = lev[lev_base(h) + p]
            lhs = jnp.concatenate([split(x[:, 64:]), split(x[:, :64])], axis=0)
            w = ls[pl.ds(LEAVES - 2 * (LEAVES >> h) + 2 * p, 2)].reshape(128, 64)
            o = dot_nt(lhs, w)
            sib[lev_base(h) + p] = jnp.where(first_half, o[0:16] + o[16:32], o[32:48] + o[48:64])

        group = min(count, 8)

        def sib_step(g, carry, sib_one=sib_one, group=group):
            for u in range(group):
                sib_one(g * group + u)
            return carry

        lax.fori_loop(0, count // group, sib_step, 0)

    target = nt_v[...] - leaf_first
    slot = lax.broadcasted_iota(jnp.int32, (LEAVES, SLOTS), 1)
    one_hot = (
        (jnp.broadcast_to(target, (LEAVES, SLOTS))
         == lax.broadcasted_iota(jnp.int32, (LEAVES, SLOTS), 0))
        & (slot < ncnt[0])
    ).astype(BF16)

    def sum_step(g, carry):
        for u in range(4):
            r = g * 4 + u
            x = prod[pl.ds(r * SLOT_ROWS, SLOTS), :]
            high = x.astype(BF16)
            low = (x - high.astype(F32)).astype(BF16)
            nacc[pl.ds(r, LEAVES, stride=LEAF_ROWS), :] = dot_nn(one_hot, high) + dot_nn(one_hot, low)
        return carry

    lax.fori_loop(0, RHS // 4, sum_step, 0)

    relay_second()

    def dup_part(owner, k):
        def dup_step(g, carry):
            for u in range(8):
                p = k * PART + g * 8 + u
                x = gath[owner, p]
                turned = jnp.concatenate([x[:, 64:], x[:, :64]], axis=1)
                base = owner * LEAVES + 2 * p
                dup[base] = split(jnp.where(first_half, x, turned))
                dup[base + 1] = split(jnp.where(first_half, turned, x))
            return carry

        lax.fori_loop(0, PART // 8, dup_step, 0)

    twin = 1 - core
    for k in range(CHUNKS):
        dup_part(col, k)
        dup_part(down_col, k)
        dup_part(up_col, k)
        recv(sibling, k, 0)
        dup_part(sibling, k)

    for i in range(1, ROWS):
        peer = lax.rem(row + ROWS - i, ROWS)
        pltpu.make_async_remote_copy(
            zr.at[peer], zr.at[peer], zr_s.at[i], zr_r.at[i],
            device_id=(peer, col), device_id_type=MESH).wait_recv()
    for i in range(8):
        upair[7 + i] = zr[2 * i] + zr[2 * i + 1]
    up_upper(7, 8, 15, 16)
    up_upper(15, 4, 19, 32)
    up_upper(19, 2, 21, 40)

    own = []
    for j, base in enumerate((0, 4, 6, 7, 15, 19, 21)):
        own.append((base, col // (1 << j)) if j < 3 else (base, row // (1 << (j - 3))))
    y = jnp.zeros((RHS, RANK), F32)
    for j in range(6, -1, -1):
        base, mine = own[j]
        pair = upair[base + mine // 2]
        turned = jnp.concatenate([pair[:, 64:], pair[:, :64]], axis=1)
        other = jnp.where(lax.rem(mine, 2) == 1, pair, turned)[:, :64]
        y = joined(dot_nt(split(other), su[j])) + joined(dot_nt(split(y), eu[48 + j]))

    relay_far()

    ylev[30] = placed(y, 0)
    for h in range(HEIGHT - 1, -1, -1):
        count = PAIRS >> h
        off = level_offset(h)

        def down_one(parent, p, h=h, off=off):
            w = mb[pl.ds(off + 2 * p, 2)].reshape(128, 64)
            value = joined(dot_nt(split(parent), w))
            if h:
                ylev[lev_base(h) + p] = value + sib[lev_base(h) + p]
            else:
                carried[p] = value

        if h == HEIGHT - 1:
            down_one(y, 0)
            continue

        def down_two(q, h=h, down_one=down_one):
            pair = ylev[lev_base(h + 1) + q]
            down_one(pair[:, :64], 2 * q)
            down_one(pair[:, 64:], 2 * q + 1)

        half = count // 2
        group = min(half, 8)

        def down_step(g, carry, down_two=down_two, group=group):
            for u in range(group):
                down_two(g * group + u)
            return carry

        lax.fori_loop(0, half // group, down_step, 0)

    for k in range(CHUNKS):
        recv(zprev * 2 + twin, k, 4)
        dup_part(zprev * 2 + twin, k)
        recv(znext * 2 + twin, k, 5)
        dup_part(znext * 2 + twin, k)
    for k in range(CHUNKS):
        dup_part(far_col, k)
    for k in range(CHUNKS):
        recv(zfar * 2 + twin, k, 6)
        dup_part(zfar * 2 + twin, k)

    bt_c.wait()
    group_first = row * (LEAVES * COLS)

    def final_step(g, carry):
        pairs = [g * (FINAL // 2) + u for u in range(FINAL // 2)]

        def listed_of(t):
            d = [dup[jnp.clip(lsrc[j, t] - group_first, 0, LEAVES * COLS - 1)]
                 for j in range(PARTNERS)]
            return jnp.concatenate(
                [jnp.where(first_half2, d[0], d[1]), jnp.where(first_half2, d[2], d[3])], axis=1)

        lhs = [jnp.concatenate([listed_of(2 * q), listed_of(2 * q + 1)], axis=0) for q in pairs]
        listed = [dot_nt(x, cp[pl.ds(2 * q, 2)].reshape(128, 256)) for x, q in zip(lhs, pairs)]
        y0 = []
        for o, q in zip(listed, pairs):
            c = carried[q]
            one = jnp.where(first_half, joined(o[:32]) + c, 0.0)
            two = jnp.where(first_half, 0.0, joined(o[32:]) + c)
            y0.append(jnp.concatenate([split(one), split(two)], axis=0))
        starts = [pl.multiple_of(q * 2 * LEAF, 2 * LEAF) for q in pairs]
        far = []
        for y, start in zip(y0, starts):
            w = bt[:, pl.ds(start, 2 * LEAF)]
            far.append(dot_nn(y, jnp.concatenate([w[:, :LEAF], w[:, LEAF:]], axis=0)))
        for o, q, start in zip(far, pairs, starts):
            out[:, pl.ds(start, 2 * LEAF)] = jnp.concatenate(
                [joined(o[:32]) + nacc[pl.ds(2 * q * LEAF_ROWS, RHS), :],
                 joined(o[32:]) + nacc[pl.ds((2 * q + 1) * LEAF_ROWS, RHS), :]], axis=1)
        return carry

    lax.fori_loop(0, LEAVES // FINAL, final_step, 0)
    halo_next.wait_send()
    halo_prev.wait_send()
    for c in sends + xr_copies + zr_copies:
        c.wait_send()


def shards(
    emission, basis_source, basis_target, local_transfer, local_sibling, upper_transfer,
    upper_sibling, leaf_source, leaf_coupling, near_block, near_target, near_source, near_count,
):
    hbm = pl.BlockSpec(memory_space=pl.ANY)
    smem = pl.BlockSpec(memory_space=pltpu.SMEM)
    vmem = pl.BlockSpec(memory_space=pltpu.VMEM)
    dma = pltpu.SemaphoreType.DMA
    V = pltpu.VMEM
    return pl.pallas_call(
        kernel,
        out_shape=V((RHS, LEAVES * LEAF), F32),
        in_specs=[hbm] * 7 + [smem, hbm, hbm, vmem, smem, smem],
        out_specs=vmem,
        scratch_shapes=[
            V((RHS, 8192), F32), V((RANK, 8192), BF16), V((RANK, 8192), BF16),
            V((64, 64, 126), BF16), V((62, 64, 64), BF16),
            V((64, 64, 254), BF16), V((64, 64, 254), BF16),
            V((LEAVES, PARTNERS, 64, 64), BF16), V((SLOTS, 128, 128), BF16),
            V((LEAVES + 2, 32, 128), BF16),
            V((2, RHS, 128), F32),
            V((COLS, PAIRS, RHS, 128), F32),
            V((COLS * LEAVES, 32, 128), BF16),
            V((128 * MAT, 128), F32),
            V((126, 64, 64), BF16),
            V((64 * MAT, 128), F32),
            V((64, 64, 64), BF16),
            V((8, 64, 64), BF16),
            V((32, RHS, 128), F32),
            V((32, RHS, 128), F32),
            V((32, RHS, 128), F32),
            V((PAIRS, RHS, 128), F32),
            V((COLS, RHS, 128), F32),
            V((ROWS, RHS, 128), F32),
            V((22, RHS, 128), F32),
            V((RHS * SLOT_ROWS, 128), F32),
            V((LEAVES * LEAF_ROWS, 128), F32),
            V((LEAVES, 64, 256), BF16),
            dma((6,)), dma((NEAR_PARTS,)), dma((NEAR_PARTS,)), dma((CHUNKS,)), dma((2,)), dma((2,)),
            dma((3, CHUNKS)), dma((4, CHUNKS)), dma((7, CHUNKS)),
            dma((COLS,)), dma((COLS,)), dma((ROWS,)), dma((ROWS,)),
        ],
        compiler_params=pltpu.CompilerParams(
            collective_id=0, has_side_effects=True, vmem_limit_bytes=58 * 1024 * 1024),
        name="h2_product",
    )(
        emission, basis_source, basis_target, local_transfer.transpose(1, 2, 0), local_sibling,
        upper_transfer.transpose(1, 2, 0), upper_sibling.transpose(1, 2, 0), leaf_source.T,
        leaf_coupling, near_block, near_target.reshape(1, SLOTS), near_source, near_count,
    )


def solution(mesh):
    both = ("row", "col")
    in_specs = (
        P(None, both), P(None, both), P(None, both), P(both, None, None), P(both, None, None),
        P(), P(), P(both, None), P(both, None, None, None), P(both, None, None),
        P(both), P(both), P(both),
    )
    return jax.shard_map(
        shards, mesh=mesh, in_specs=in_specs, out_specs=P(None, both), check_vma=False)
```

```python
import functools

import jax
import jax.numpy as jnp
from jax import lax
from jax.experimental import pallas as pl
from jax.experimental.pallas import tpu as pltpu
from jax.sharding import PartitionSpec as P

MESH = pl.DeviceIdType.MESH
F32 = jnp.float32
BF16 = jnp.bfloat16

RHS = 16
RANK = 64
LEAF = 128
LEAVES = 64
PAIRS = LEAVES // 2
PARTNERS = 4
SLOTS = 192
ROWS, COLS = 16, 8
CHUNKS = 2
PART = PAIRS // CHUNKS
HEIGHT = 6
NEAR_PARTS = 4
FINAL = 16
MAT, SLOT_ROWS, LEAF_ROWS = 33, SLOTS + 1, RHS + 1


def dot_nn(a, b):
    return lax.dot_general(a, b, (((1,), (0,)), ((), ())), preferred_element_type=F32)


def dot_nt(a, b):
    return lax.dot_general(a, b, (((1,), (1,)), ((), ())), preferred_element_type=F32)


def split(x):
    high = x.astype(BF16)
    low = (x - high.astype(F32)).astype(BF16)
    return jnp.concatenate([high, low], axis=0)


def joined(o):
    half = o.shape[0] // 2
    return o[:half] + o[half:]


def level_offset(h):
    return 2 * LEAVES - 2 * (LEAVES >> h)


def lev_base(h):
    return PAIRS - (PAIRS >> (h - 1)) if h >= 1 else 0


def kernel(
    em_h, bs_h, bt_h, lt_h, ls_h, ut_h, us_h, lsrc, lc_h, nb_h, nt_v, nsrc, ncnt,
    out,
    em, bs, bt, lt, ls, ut, us, lc, nb,
    eh, halo, gath, dup, mp, mb, mu, eu, su, lev, sib, ylev, carried,
    xr, zr, upair, prod, nacc, cp,
    load_sem, nb_sem, lc_sem, bs_sem, halo_s, halo_r,
    own_s, fwd_s, gath_r, xr_s, xr_r, zr_s, zr_r,
):
    row, col = lax.axis_index("row"), lax.axis_index("col")
    device = row * COLS + col
    z, core = col // 2, col % 2
    sibling = z * 2 + 1 - core
    znext = lax.rem(z + 1, 4)
    zprev = lax.rem(z + 3, 4)
    zfar = lax.rem(z + 2, 4)
    up_col, down_col, far_col = znext * 2 + core, zprev * 2 + core, zfar * 2 + core

    def load(src, dst, i):
        c = pltpu.make_async_copy(src, dst, load_sem.at[i])
        c.start()
        return c

    em_c = load(em_h, em, 0)
    width = 8192 // CHUNKS
    bs_c = []
    for k in range(CHUNKS):
        c = pltpu.make_async_copy(
            bs_h.at[:, pl.ds(k * width, width)], bs.at[:, pl.ds(k * width, width)], bs_sem.at[k]
        )
        c.start()
        bs_c.append(c)

    barrier = pltpu.get_barrier_semaphore()
    nxt, prv = lax.rem(device + 1, ROWS * COLS), lax.rem(device + ROWS * COLS - 1, ROWS * COLS)
    next_id = (nxt // COLS, lax.rem(nxt, COLS))
    prev_id = (prv // COLS, lax.rem(prv, COLS))
    for i in range(1, COLS):
        pl.semaphore_signal(barrier, 1, device_id=(row, lax.rem(col + i, COLS)), device_id_type=MESH)
    for i in range(1, ROWS):
        pl.semaphore_signal(barrier, 1, device_id=(lax.rem(row + i, ROWS), col), device_id_type=MESH)
    pl.semaphore_signal(barrier, 1, device_id=next_id, device_id_type=MESH)
    pl.semaphore_signal(barrier, 1, device_id=prev_id, device_id_type=MESH)

    per, lper = SLOTS // NEAR_PARTS, LEAVES // NEAR_PARTS

    def load_near(k):
        pltpu.make_async_copy(
            nb_h.at[pl.ds(k * per, per)], nb.at[pl.ds(k * per, per)], nb_sem.at[k]).start()
        pltpu.make_async_copy(
            lc_h.at[pl.ds(k * lper, lper)], lc.at[pl.ds(k * lper, lper)], lc_sem.at[k]).start()

    lane = lax.broadcasted_iota(jnp.int32, (RHS, 128), 1)
    first_half = lane < 64
    lane2 = lax.broadcasted_iota(jnp.int32, (2 * RHS, 128), 1)
    first_half2 = lane2 < 64

    em_c.wait()
    lt_c = load(lt_h, lt, 1)

    def split_leaf(g, carry):
        for u in range(8):
            l = g * 8 + u
            eh[l + 1] = split(em[:, pl.ds(pl.multiple_of(l * LEAF, LEAF), LEAF)])
        return carry

    lax.fori_loop(0, LEAVES // 8, split_leaf, 0)

    def piece(owner, k):
        return gath.at[owner, pl.ds(k * PART, PART)]

    def send(owner, k, to_col, send_sem, kind):
        return pltpu.make_async_remote_copy(
            piece(owner, k), piece(owner, k), send_sem, gath_r.at[kind, k],
            device_id=(row, to_col), device_id_type=MESH)

    sends = []

    def begin(owner, k, to_col, send_sem, kind):
        c = send(owner, k, to_col, send_sem, kind)
        c.start()
        sends.append(c)

    def leaf_pair(p):
        a = eh[pl.ds(2 * p + 1, 2)].reshape(64, 128)
        start = pl.multiple_of(p * 256, 256)
        w = bs[:, pl.ds(start, 256)]
        b = jnp.concatenate([w[:, :128], w[:, 128:]], axis=0)
        o = dot_nt(a, b)
        gath[col, p] = jnp.where(first_half, o[0:16] + o[16:32], o[32:48] + o[48:64])

    for k in range(CHUNKS):
        bs_c[k].wait()

        def leaf_step(g, carry, k=k):
            for u in range(8):
                leaf_pair(k * PART + g * 8 + u)
            return carry

        lax.fori_loop(0, PART // 8, leaf_step, 0)

    def recv(owner, k, kind):
        pltpu.make_async_remote_copy(
            piece(owner, k), piece(owner, k), own_s.at[0, k], gath_r.at[kind, k],
            device_id=(row, col), device_id_type=MESH).wait_recv()

    def relay_first():
        recv(down_col, 0, 1)
        begin(down_col, 0, up_col, fwd_s.at[0, 0], 3)
        recv(up_col, 1, 2)
        begin(up_col, 1, down_col, fwd_s.at[0, 1], 3)
        begin(down_col, 0, sibling, fwd_s.at[1, 0], 4)
        begin(up_col, 1, sibling, fwd_s.at[2, 1], 5)

    def relay_second():
        recv(down_col, 1, 1)
        begin(down_col, 1, sibling, fwd_s.at[1, 1], 4)
        recv(up_col, 0, 2)
        begin(up_col, 0, sibling, fwd_s.at[2, 0], 5)

    def relay_far():
        for k in range(CHUNKS):
            recv(far_col, k, 3)
            begin(far_col, k, sibling, fwd_s.at[3, k], 6)

    ut_c = load(ut_h, ut, 2)
    us_c = load(us_h, us, 3)
    lt_c.wait()
    load_near(0)
    ls_c = load(ls_h, ls, 4)
    for k in range(1, NEAR_PARTS):
        load_near(k)
    bt_c = load(bt_h, bt, 5)
    eye = (
        lax.broadcasted_iota(jnp.int32, (128, 126), 0)
        == lax.broadcasted_iota(jnp.int32, (128, 126), 1)
    ).astype(BF16)

    def turn_local(q, carry):
        w = jnp.concatenate([lt[q], lt[q + 32]], axis=0)
        mp[pl.ds(q, 128, stride=MAT), :] = dot_nt(eye, w)
        return carry

    lax.fori_loop(0, 32, turn_local, 0, unroll=4)

    def unpack(source, target, n):
        m = source[pl.ds(n * MAT, 32), :].astype(BF16)
        target[n] = jnp.concatenate([m[:, :64], m[:, 64:]], axis=0)

    def unpack_local(g, carry):
        for u in range(18):
            unpack(mp, mb, g * 18 + u)
        return carry

    lax.fori_loop(0, 7, unpack_local, 0)

    def lift(pair, weights):
        return joined(dot_nn(split(pair), weights.reshape(128, 64)))

    zero = jnp.zeros((2 * RHS, LEAF), BF16)

    def lift_two(one, two, weights):
        lhs = jnp.concatenate(
            [jnp.concatenate([split(one), zero], axis=1),
             jnp.concatenate([zero, split(two)], axis=1)], axis=0)
        o = dot_nn(lhs, weights.reshape(256, 64))
        return jnp.concatenate([joined(o[:32]), joined(o[32:])], axis=1)

    def level_pair(h, p):
        return gath[col, p] if h == 0 else lev[lev_base(h) + p]

    for h in range(HEIGHT - 1):
        count = PAIRS >> h
        off = level_offset(h)

        def up_two(q, h=h, off=off):
            lev[lev_base(h + 1) + q] = lift_two(
                level_pair(h, 2 * q), level_pair(h, 2 * q + 1), mb[pl.ds(off + 4 * q, 4)])

        half = count // 2
        group = min(half, 8)

        def up_step(g, carry, up_two=up_two, group=group):
            for u in range(group):
                up_two(g * group + u)
            return carry

        lax.fori_loop(0, half // group, up_step, 0)
    root = lift(lev[lev_base(5)], mb[pl.ds(level_offset(5), 2)])

    def placed(value, parity):
        return jnp.where(
            (lane >= 64).astype(jnp.int32) == parity, jnp.concatenate([value, value], axis=1), 0.0
        )

    xr[col] = placed(root, core)
    pl.semaphore_wait(barrier, COLS - 1 + ROWS - 1 + 2)

    halo_next = pltpu.make_async_remote_copy(
        em.at[:, pl.ds((LEAVES - 1) * LEAF, LEAF)], halo.at[0], halo_s.at[0], halo_r.at[0],
        device_id=next_id, device_id_type=MESH)
    halo_prev = pltpu.make_async_remote_copy(
        em.at[:, pl.ds(0, LEAF)], halo.at[1], halo_s.at[1], halo_r.at[1],
        device_id=prev_id, device_id_type=MESH)
    halo_next.start()
    halo_prev.start()

    xr_copies = []
    for i in range(1, COLS):
        c = pltpu.make_async_remote_copy(
            xr.at[col], xr.at[col], xr_s.at[i], xr_r.at[i],
            device_id=(row, lax.rem(col + i, COLS)), device_id_type=MESH)
        c.start()
        xr_copies.append(c)

    begin(col, 0, up_col, own_s.at[0, 0], 1)
    begin(col, 1, down_col, own_s.at[1, 1], 2)
    for k in range(CHUNKS):
        begin(col, k, sibling, own_s.at[2, k], 0)
    begin(col, 1, up_col, own_s.at[0, 1], 1)
    begin(col, 0, down_col, own_s.at[1, 0], 2)

    ut_c.wait()
    us_c.wait()
    picks = lax.broadcasted_iota(jnp.int32, (64, 254), 0)
    cluster = lax.broadcasted_iota(jnp.int32, (64, 254), 1)
    want = jnp.where(picks < 8, row * 8 + picks, -1)
    want = jnp.where((picks >= 8) & (picks < 12), 128 + row * 4 + picks - 8, want)
    want = jnp.where((picks >= 12) & (picks < 14), 192 + row * 2 + picks - 12, want)
    want = jnp.where((picks >= 16) & (picks < 46), 224 + picks - 16, want)
    for j in range(7):
        want = jnp.where(picks == 48 + j, 256 - (256 >> j) + (device // (1 << j)), want)
    pick_u = (cluster == want).astype(BF16)
    picks_s = lax.broadcasted_iota(jnp.int32, (16, 254), 0)
    cluster_s = lax.broadcasted_iota(jnp.int32, (16, 254), 1)
    want_s = jnp.full((16, 254), -1, jnp.int32)
    for j in range(7):
        want_s = jnp.where(picks_s == j, 256 - (256 >> j) + (device // (1 << j)), want_s)
    pick_s = (cluster_s == want_s).astype(BF16)

    def turn_upper(q, carry):
        w = jnp.concatenate([ut[q], ut[q + 32]], axis=0)
        mu[pl.ds(q, 64, stride=MAT), :] = dot_nt(pick_u, w)
        w = jnp.concatenate([us[q], us[q + 32]], axis=0)
        mp[pl.ds(q, 16, stride=MAT), :] = dot_nt(pick_s, w)
        return carry

    lax.fori_loop(0, 32, turn_upper, 0, unroll=4)

    def unpack_upper(g, carry):
        for u in range(16):
            unpack(mu, eu, g * 16 + u)
        for u in range(2):
            unpack(mp, su, g * 2 + u)
        return carry

    lax.fori_loop(0, 4, unpack_upper, 0)

    halo_next.wait_recv()
    halo_prev.wait_recv()
    eh[0] = split(halo[0])
    eh[LEAVES + 1] = split(halo[1])
    leaf_first = device * LEAVES
    def sib_one(i):
        x = lev[i]
        lhs = jnp.concatenate([split(x[:, 64:]), split(x[:, :64])], axis=0)
        o = dot_nt(lhs, ls[pl.ds(2 * i, 2)].reshape(128, 64))
        sib[i] = jnp.where(first_half, o[0:16] + o[16:32], o[32:48] + o[48:64])

    ls_c.wait()

    def near_part(k):
        pltpu.make_async_copy(
            nb_h.at[pl.ds(k * per, per)], nb.at[pl.ds(k * per, per)], nb_sem.at[k]).wait()
        pltpu.make_async_copy(
            lc_h.at[pl.ds(k * lper, lper)], lc.at[pl.ds(k * lper, lper)], lc_sem.at[k]).wait()

        def near_step(g, carry):
            for u in range(12):
                s = k * per + g * 24 + 2 * u
                one, two = (
                    eh[jnp.clip(nsrc[s + i] - leaf_first + 1, 0, LEAVES + 1)] for i in range(2))
                lhs = jnp.concatenate(
                    [jnp.concatenate([one, zero], axis=1), jnp.concatenate([zero, two], axis=1)],
                    axis=0)
                o = dot_nt(lhs, jnp.concatenate([nb[s], nb[s + 1]], axis=1))
                prod[pl.ds(s, RHS, stride=SLOT_ROWS), :] = joined(o[:32])
                prod[pl.ds(s + 1, RHS, stride=SLOT_ROWS), :] = joined(o[32:])
                if u < 4:
                    sib_one(lax.rem((2 * k + g) * 4 + u, PAIRS - 1))
                if u < 8:
                    t = k * lper + g * 8 + u
                    cp[t] = jnp.concatenate([lc[t, 0], lc[t, 1], lc[t, 2], lc[t, 3]], axis=1)
            return carry

        lax.fori_loop(0, per // 24, near_step, 0)

    near_part(0)

    for i in range(1, COLS):
        peer = lax.rem(col + COLS - i, COLS)
        pltpu.make_async_remote_copy(
            xr.at[peer], xr.at[peer], xr_s.at[i], xr_r.at[i],
            device_id=(row, peer), device_id_type=MESH).wait_recv()
    for i in range(4):
        upair[i] = xr[2 * i] + xr[2 * i + 1]

    def up_upper(source, count, target, first):
        for i in range(count // 2):
            upair[target + i] = lift_two(
                upair[source + 2 * i], upair[source + 2 * i + 1],
                eu[first + 4 * i : first + 4 * i + 4])

    up_upper(0, 4, 4, 0)
    up_upper(4, 2, 6, 8)
    row_root = lift(upair[6], eu[12:14])
    zr[row] = placed(row_root, lax.rem(row, 2))
    zr_copies = []
    for i in range(1, ROWS):
        c = pltpu.make_async_remote_copy(
            zr.at[row], zr.at[row], zr_s.at[i], zr_r.at[i],
            device_id=(lax.rem(row + i, ROWS), col), device_id_type=MESH)
        c.start()
        zr_copies.append(c)

    near_part(1)
    near_part(2)
    relay_first()
    near_part(3)

    target = nt_v[...] - leaf_first
    slot = lax.broadcasted_iota(jnp.int32, (LEAVES, SLOTS), 1)
    one_hot = (
        (jnp.broadcast_to(target, (LEAVES, SLOTS))
         == lax.broadcasted_iota(jnp.int32, (LEAVES, SLOTS), 0))
        & (slot < ncnt[0])
    ).astype(BF16)

    relay_second()

    def dup_pair(owner, p):
        x = gath[owner, p]
        turned = jnp.concatenate([x[:, 64:], x[:, :64]], axis=1)
        base = owner * LEAVES + 2 * p
        dup[base] = split(jnp.where(first_half, x, turned))
        dup[base + 1] = split(jnp.where(first_half, turned, x))

    def dup_all(owner):
        def dup_step(g, carry):
            for u in range(16):
                dup_pair(owner, g * 16 + u)
            return carry

        lax.fori_loop(0, PAIRS // 16, dup_step, 0)

    twin = 1 - core
    for k in range(CHUNKS):
        recv(sibling, k, 0)
    for first, owner in ((0, col), (4, down_col), (8, up_col), (12, sibling)):

        def sum_step(g, carry, first=first, owner=owner):
            for u in range(2):
                r = first + g * 2 + u
                x = prod[pl.ds(r * SLOT_ROWS, SLOTS), :]
                high = x.astype(BF16)
                low = (x - high.astype(F32)).astype(BF16)
                nacc[pl.ds(r, LEAVES, stride=LEAF_ROWS), :] = (
                    dot_nn(one_hot, high) + dot_nn(one_hot, low))
                for v in range(8):
                    dup_pair(owner, g * 16 + u * 8 + v)
            return carry

        lax.fori_loop(0, 2, sum_step, 0)
    for kind, owner in ((4, zprev * 2 + twin), (5, znext * 2 + twin)):
        for k in range(CHUNKS):
            recv(owner, k, kind)
        dup_all(owner)
    relay_far()
    dup_all(far_col)

    for i in range(1, ROWS):
        peer = lax.rem(row + ROWS - i, ROWS)
        pltpu.make_async_remote_copy(
            zr.at[peer], zr.at[peer], zr_s.at[i], zr_r.at[i],
            device_id=(peer, col), device_id_type=MESH).wait_recv()
    for i in range(8):
        upair[7 + i] = zr[2 * i] + zr[2 * i + 1]
    up_upper(7, 8, 15, 16)
    up_upper(15, 4, 19, 32)
    up_upper(19, 2, 21, 40)

    own = []
    for j, base in enumerate((0, 4, 6, 7, 15, 19, 21)):
        own.append((base, col // (1 << j)) if j < 3 else (base, row // (1 << (j - 3))))
    y = jnp.zeros((RHS, RANK), F32)
    for j in range(6, -1, -1):
        base, mine = own[j]
        pair = upair[base + mine // 2]
        turned = jnp.concatenate([pair[:, 64:], pair[:, :64]], axis=1)
        other = jnp.where(lax.rem(mine, 2) == 1, pair, turned)[:, :64]
        y = joined(dot_nt(split(other), su[j])) + joined(dot_nt(split(y), eu[48 + j]))

    ylev[30] = placed(y, 0)
    for h in range(HEIGHT - 1, -1, -1):
        count = PAIRS >> h
        off = level_offset(h)

        def down_one(parent, p, h=h, off=off):
            w = mb[pl.ds(off + 2 * p, 2)].reshape(128, 64)
            value = joined(dot_nt(split(parent), w))
            if h:
                ylev[lev_base(h) + p] = value + sib[lev_base(h) + p]
            else:
                carried[p] = value

        if h == HEIGHT - 1:
            down_one(y, 0)
            continue

        def down_two(q, h=h, down_one=down_one):
            pair = ylev[lev_base(h + 1) + q]
            down_one(pair[:, :64], 2 * q)
            down_one(pair[:, 64:], 2 * q + 1)

        half = count // 2
        group = min(half, 8)

        def down_step(g, carry, down_two=down_two, group=group):
            for u in range(group):
                down_two(g * group + u)
            return carry

        lax.fori_loop(0, half // group, down_step, 0)

    for k in range(CHUNKS):
        recv(zfar * 2 + twin, k, 6)
    dup_all(zfar * 2 + twin)

    bt_c.wait()
    group_first = row * (LEAVES * COLS)

    def final_step(g, carry):
        pairs = [g * (FINAL // 2) + u for u in range(FINAL // 2)]

        def listed_of(t):
            d = [dup[jnp.clip(lsrc[j, t] - group_first, 0, LEAVES * COLS - 1)]
                 for j in range(PARTNERS)]
            return jnp.concatenate(
                [jnp.where(first_half2, d[0], d[1]), jnp.where(first_half2, d[2], d[3])], axis=1)

        lhs = [jnp.concatenate([listed_of(2 * q), listed_of(2 * q + 1)], axis=0) for q in pairs]
        listed = [dot_nt(x, cp[pl.ds(2 * q, 2)].reshape(128, 256)) for x, q in zip(lhs, pairs)]
        y0 = []
        for o, q in zip(listed, pairs):
            c = carried[q]
            one = jnp.where(first_half, joined(o[:32]) + c, 0.0)
            two = jnp.where(first_half, 0.0, joined(o[32:]) + c)
            y0.append(jnp.concatenate([split(one), split(two)], axis=0))
        starts = [pl.multiple_of(q * 2 * LEAF, 2 * LEAF) for q in pairs]
        far = []
        for y, start in zip(y0, starts):
            w = bt[:, pl.ds(start, 2 * LEAF)]
            far.append(dot_nn(y, jnp.concatenate([w[:, :LEAF], w[:, LEAF:]], axis=0)))
        for o, q, start in zip(far, pairs, starts):
            out[:, pl.ds(start, 2 * LEAF)] = jnp.concatenate(
                [joined(o[:32]) + nacc[pl.ds(2 * q * LEAF_ROWS, RHS), :],
                 joined(o[32:]) + nacc[pl.ds((2 * q + 1) * LEAF_ROWS, RHS), :]], axis=1)
        return carry

    lax.fori_loop(0, LEAVES // FINAL, final_step, 0)
    halo_next.wait_send()
    halo_prev.wait_send()
    for c in sends + xr_copies + zr_copies:
        c.wait_send()


def shards(
    emission, basis_source, basis_target, local_transfer, local_sibling, upper_transfer,
    upper_sibling, leaf_source, leaf_coupling, near_block, near_target, near_source, near_count,
):
    hbm = pl.BlockSpec(memory_space=pl.ANY)
    smem = pl.BlockSpec(memory_space=pltpu.SMEM)
    vmem = pl.BlockSpec(memory_space=pltpu.VMEM)
    dma = pltpu.SemaphoreType.DMA
    V = pltpu.VMEM
    return pl.pallas_call(
        kernel,
        out_shape=V((RHS, LEAVES * LEAF), F32),
        in_specs=[hbm] * 7 + [smem, hbm, hbm, vmem, smem, smem],
        out_specs=vmem,
        scratch_shapes=[
            V((RHS, 8192), F32), V((RANK, 8192), BF16), V((RANK, 8192), BF16),
            V((64, 64, 126), BF16), V((62, 64, 64), BF16),
            V((64, 64, 254), BF16), V((64, 64, 254), BF16),
            V((LEAVES, PARTNERS, 64, 64), BF16), V((SLOTS, 128, 128), BF16),
            V((LEAVES + 2, 32, 128), BF16),
            V((2, RHS, 128), F32),
            V((COLS, PAIRS, RHS, 128), F32),
            V((COLS * LEAVES, 32, 128), BF16),
            V((128 * MAT, 128), F32),
            V((126, 64, 64), BF16),
            V((64 * MAT, 128), F32),
            V((64, 64, 64), BF16),
            V((8, 64, 64), BF16),
            V((32, RHS, 128), F32),
            V((32, RHS, 128), F32),
            V((32, RHS, 128), F32),
            V((PAIRS, RHS, 128), F32),
            V((COLS, RHS, 128), F32),
            V((ROWS, RHS, 128), F32),
            V((22, RHS, 128), F32),
            V((RHS * SLOT_ROWS, 128), F32),
            V((LEAVES * LEAF_ROWS, 128), F32),
            V((LEAVES, 64, 256), BF16),
            dma((6,)), dma((NEAR_PARTS,)), dma((NEAR_PARTS,)), dma((CHUNKS,)), dma((2,)), dma((2,)),
            dma((3, CHUNKS)), dma((4, CHUNKS)), dma((7, CHUNKS)),
            dma((COLS,)), dma((COLS,)), dma((ROWS,)), dma((ROWS,)),
        ],
        compiler_params=pltpu.CompilerParams(
            collective_id=0, has_side_effects=True, vmem_limit_bytes=58 * 1024 * 1024),
        name="h2_product",
    )(
        emission, basis_source, basis_target, local_transfer.transpose(1, 2, 0), local_sibling,
        upper_transfer.transpose(1, 2, 0), upper_sibling.transpose(1, 2, 0), leaf_source.T,
        leaf_coupling, near_block, near_target.reshape(1, SLOTS), near_source, near_count,
    )


def solution(mesh):
    both = ("row", "col")
    in_specs = (
        P(None, both), P(None, both), P(None, both), P(both, None, None), P(both, None, None),
        P(), P(), P(both, None), P(both, None, None, None), P(both, None, None),
        P(both), P(both), P(both),
    )
    return jax.shard_map(
        shards, mesh=mesh, in_specs=in_specs, out_specs=P(None, both), check_vma=False)
```

```python
import functools

import jax
import jax.numpy as jnp
from jax import lax
from jax.experimental import pallas as pl
from jax.experimental.pallas import tpu as pltpu
from jax.sharding import PartitionSpec as P

MESH = pl.DeviceIdType.MESH
F32 = jnp.float32
BF16 = jnp.bfloat16

RHS = 16
RANK = 64
LEAF = 128
LEAVES = 64
PAIRS = LEAVES // 2
PARTNERS = 4
SLOTS = 192
ROWS, COLS = 16, 8
CHUNKS = 2
PART = PAIRS // CHUNKS
HEIGHT = 6
NEAR_PARTS = 4
FINAL = 16
MAT, SLOT_ROWS, LEAF_ROWS = 33, SLOTS + 1, RHS + 1


def dot_nn(a, b):
    return lax.dot_general(a, b, (((1,), (0,)), ((), ())), preferred_element_type=F32)


def dot_nt(a, b):
    return lax.dot_general(a, b, (((1,), (1,)), ((), ())), preferred_element_type=F32)


def split(x):
    high = x.astype(BF16)
    low = (x - high.astype(F32)).astype(BF16)
    return jnp.concatenate([high, low], axis=0)


def joined(o):
    half = o.shape[0] // 2
    return o[:half] + o[half:]


def level_offset(h):
    return 2 * LEAVES - 2 * (LEAVES >> h)


def lev_base(h):
    return PAIRS - (PAIRS >> (h - 1)) if h >= 1 else 0


def kernel(
    em_h, bs_h, bt_h, lt_h, ls_h, ut_h, us_h, lsrc, lc_h, nb_h, nt_v, nsrc, ncnt,
    out,
    em, bs, bt, lt, ls, ut, us, lc, nb,
    eh, halo, gath, dup, mp, mb, mu, eu, su, lev, sib, ylev, carried,
    xr, zr, upair, prod, nacc, cp,
    load_sem, nb_sem, lc_sem, bs_sem, halo_s, halo_r,
    own_s, fwd_s, gath_r, xr_s, xr_r, zr_s, zr_r,
):
    row, col = lax.axis_index("row"), lax.axis_index("col")
    device = row * COLS + col
    z, core = col // 2, col % 2
    sibling = z * 2 + 1 - core
    znext = lax.rem(z + 1, 4)
    zprev = lax.rem(z + 3, 4)
    zfar = lax.rem(z + 2, 4)
    up_col, down_col, far_col = znext * 2 + core, zprev * 2 + core, zfar * 2 + core

    def load(src, dst, i):
        c = pltpu.make_async_copy(src, dst, load_sem.at[i])
        c.start()
        return c

    em_c = load(em_h, em, 0)
    width = 8192 // CHUNKS
    bs_c = []
    for k in range(CHUNKS):
        c = pltpu.make_async_copy(
            bs_h.at[:, pl.ds(k * width, width)], bs.at[:, pl.ds(k * width, width)], bs_sem.at[k]
        )
        c.start()
        bs_c.append(c)

    barrier = pltpu.get_barrier_semaphore()
    nxt, prv = lax.rem(device + 1, ROWS * COLS), lax.rem(device + ROWS * COLS - 1, ROWS * COLS)
    next_id = (nxt // COLS, lax.rem(nxt, COLS))
    prev_id = (prv // COLS, lax.rem(prv, COLS))
    for i in range(1, COLS):
        pl.semaphore_signal(barrier, 1, device_id=(row, lax.rem(col + i, COLS)), device_id_type=MESH)
    for i in range(1, ROWS):
        pl.semaphore_signal(barrier, 1, device_id=(lax.rem(row + i, ROWS), col), device_id_type=MESH)
    pl.semaphore_signal(barrier, 1, device_id=next_id, device_id_type=MESH)
    pl.semaphore_signal(barrier, 1, device_id=prev_id, device_id_type=MESH)

    per, lper = SLOTS // NEAR_PARTS, LEAVES // NEAR_PARTS

    def load_near(k):
        pltpu.make_async_copy(
            nb_h.at[pl.ds(k * per, per)], nb.at[pl.ds(k * per, per)], nb_sem.at[k]).start()
        pltpu.make_async_copy(
            lc_h.at[pl.ds(k * lper, lper)], lc.at[pl.ds(k * lper, lper)], lc_sem.at[k]).start()

    lane = lax.broadcasted_iota(jnp.int32, (RHS, 128), 1)
    first_half = lane < 64
    lane2 = lax.broadcasted_iota(jnp.int32, (2 * RHS, 128), 1)
    first_half2 = lane2 < 64

    em_c.wait()
    lt_c = load(lt_h, lt, 1)

    def split_leaf(g, carry):
        for u in range(8):
            l = g * 8 + u
            eh[l + 1] = split(em[:, pl.ds(pl.multiple_of(l * LEAF, LEAF), LEAF)])
        return carry

    lax.fori_loop(0, LEAVES // 8, split_leaf, 0)

    def piece(owner, k):
        return gath.at[owner, pl.ds(k * PART, PART)]

    def send(owner, k, to_col, send_sem, kind):
        return pltpu.make_async_remote_copy(
            piece(owner, k), piece(owner, k), send_sem, gath_r.at[kind, k],
            device_id=(row, to_col), device_id_type=MESH)

    sends = []

    def begin(owner, k, to_col, send_sem, kind):
        c = send(owner, k, to_col, send_sem, kind)
        c.start()
        sends.append(c)

    def leaf_pair(p):
        a = eh[pl.ds(2 * p + 1, 2)].reshape(64, 128)
        start = pl.multiple_of(p * 256, 256)
        w = bs[:, pl.ds(start, 256)]
        b = jnp.concatenate([w[:, :128], w[:, 128:]], axis=0)
        o = dot_nt(a, b)
        gath[col, p] = jnp.where(first_half, o[0:16] + o[16:32], o[32:48] + o[48:64])

    for k in range(CHUNKS):
        bs_c[k].wait()

        def leaf_step(g, carry, k=k):
            for u in range(8):
                leaf_pair(k * PART + g * 8 + u)
            return carry

        lax.fori_loop(0, PART // 8, leaf_step, 0)

    def recv(owner, k, kind):
        pltpu.make_async_remote_copy(
            piece(owner, k), piece(owner, k), own_s.at[0, k], gath_r.at[kind, k],
            device_id=(row, col), device_id_type=MESH).wait_recv()

    def relay_first():
        recv(down_col, 0, 1)
        begin(down_col, 0, up_col, fwd_s.at[0, 0], 3)
        recv(up_col, 1, 2)
        begin(up_col, 1, down_col, fwd_s.at[0, 1], 3)
        begin(down_col, 0, sibling, fwd_s.at[1, 0], 4)
        begin(up_col, 1, sibling, fwd_s.at[2, 1], 5)

    def relay_second():
        recv(down_col, 1, 1)
        begin(down_col, 1, sibling, fwd_s.at[1, 1], 4)
        recv(up_col, 0, 2)
        begin(up_col, 0, sibling, fwd_s.at[2, 0], 5)

    def relay_far():
        for k in range(CHUNKS):
            recv(far_col, k, 3)
            begin(far_col, k, sibling, fwd_s.at[3, k], 6)

    ut_c = load(ut_h, ut, 2)
    us_c = load(us_h, us, 3)
    lt_c.wait()
    load_near(0)
    ls_c = load(ls_h, ls, 4)
    for k in range(1, NEAR_PARTS):
        load_near(k)
    bt_c = load(bt_h, bt, 5)
    eye = (
        lax.broadcasted_iota(jnp.int32, (128, 126), 0)
        == lax.broadcasted_iota(jnp.int32, (128, 126), 1)
    ).astype(BF16)

    def turn_local(q, carry):
        w = jnp.concatenate([lt[q], lt[q + 32]], axis=0)
        mp[pl.ds(q, 128, stride=MAT), :] = dot_nt(eye, w)
        return carry

    lax.fori_loop(0, 32, turn_local, 0, unroll=4)

    def unpack(source, target, n):
        m = source[pl.ds(n * MAT, 32), :].astype(BF16)
        target[n] = jnp.concatenate([m[:, :64], m[:, 64:]], axis=0)

    def unpack_local(g, carry):
        for u in range(18):
            unpack(mp, mb, g * 18 + u)
        return carry

    lax.fori_loop(0, 7, unpack_local, 0)

    def lift(pair, weights):
        return joined(dot_nn(split(pair), weights.reshape(128, 64)))

    zero = jnp.zeros((2 * RHS, LEAF), BF16)

    def lift_two(one, two, weights):
        lhs = jnp.concatenate(
            [jnp.concatenate([split(one), zero], axis=1),
             jnp.concatenate([zero, split(two)], axis=1)], axis=0)
        o = dot_nn(lhs, weights.reshape(256, 64))
        return jnp.concatenate([joined(o[:32]), joined(o[32:])], axis=1)

    def level_pair(h, p):
        return gath[col, p] if h == 0 else lev[lev_base(h) + p]

    for h in range(HEIGHT - 1):
        count = PAIRS >> h
        off = level_offset(h)

        def up_two(q, h=h, off=off):
            lev[lev_base(h + 1) + q] = lift_two(
                level_pair(h, 2 * q), level_pair(h, 2 * q + 1), mb[pl.ds(off + 4 * q, 4)])

        half = count // 2
        group = min(half, 8)

        def up_step(g, carry, up_two=up_two, group=group):
            for u in range(group):
                up_two(g * group + u)
            return carry

        lax.fori_loop(0, half // group, up_step, 0)
    root = lift(lev[lev_base(5)], mb[pl.ds(level_offset(5), 2)])

    def placed(value, parity):
        return jnp.where(
            (lane >= 64).astype(jnp.int32) == parity, jnp.concatenate([value, value], axis=1), 0.0
        )

    xr[col] = placed(root, core)
    pl.semaphore_wait(barrier, COLS - 1 + ROWS - 1 + 2)

    halo_next = pltpu.make_async_remote_copy(
        em.at[:, pl.ds((LEAVES - 1) * LEAF, LEAF)], halo.at[0], halo_s.at[0], halo_r.at[0],
        device_id=next_id, device_id_type=MESH)
    halo_prev = pltpu.make_async_remote_copy(
        em.at[:, pl.ds(0, LEAF)], halo.at[1], halo_s.at[1], halo_r.at[1],
        device_id=prev_id, device_id_type=MESH)

    xr_copies = []
    for i in range(1, COLS):
        c = pltpu.make_async_remote_copy(
            xr.at[col], xr.at[col], xr_s.at[i], xr_r.at[i],
            device_id=(row, lax.rem(col + i, COLS)), device_id_type=MESH)
        c.start()
        xr_copies.append(c)

    halo_next.start()
    halo_prev.start()
    begin(col, 0, up_col, own_s.at[0, 0], 1)
    begin(col, 1, down_col, own_s.at[1, 1], 2)
    for k in range(CHUNKS):
        begin(col, k, sibling, own_s.at[2, k], 0)
    begin(col, 1, up_col, own_s.at[0, 1], 1)
    begin(col, 0, down_col, own_s.at[1, 0], 2)

    ut_c.wait()
    us_c.wait()
    picks = lax.broadcasted_iota(jnp.int32, (64, 254), 0)
    cluster = lax.broadcasted_iota(jnp.int32, (64, 254), 1)
    want = jnp.where(picks < 8, row * 8 + picks, -1)
    want = jnp.where((picks >= 8) & (picks < 12), 128 + row * 4 + picks - 8, want)
    want = jnp.where((picks >= 12) & (picks < 14), 192 + row * 2 + picks - 12, want)
    want = jnp.where((picks >= 16) & (picks < 46), 224 + picks - 16, want)
    for j in range(7):
        want = jnp.where(picks == 48 + j, 256 - (256 >> j) + (device // (1 << j)), want)
    pick_u = (cluster == want).astype(BF16)
    picks_s = lax.broadcasted_iota(jnp.int32, (16, 254), 0)
    cluster_s = lax.broadcasted_iota(jnp.int32, (16, 254), 1)
    want_s = jnp.full((16, 254), -1, jnp.int32)
    for j in range(7):
        want_s = jnp.where(picks_s == j, 256 - (256 >> j) + (device // (1 << j)), want_s)
    pick_s = (cluster_s == want_s).astype(BF16)

    def turn_upper(q, carry):
        w = jnp.concatenate([ut[q], ut[q + 32]], axis=0)
        mu[pl.ds(q, 64, stride=MAT), :] = dot_nt(pick_u, w)
        w = jnp.concatenate([us[q], us[q + 32]], axis=0)
        mp[pl.ds(q, 16, stride=MAT), :] = dot_nt(pick_s, w)
        return carry

    lax.fori_loop(0, 32, turn_upper, 0, unroll=4)

    def unpack_upper(g, carry):
        for u in range(16):
            unpack(mu, eu, g * 16 + u)
        for u in range(2):
            unpack(mp, su, g * 2 + u)
        return carry

    lax.fori_loop(0, 4, unpack_upper, 0)

    halo_next.wait_recv()
    halo_prev.wait_recv()
    eh[0] = split(halo[0])
    eh[LEAVES + 1] = split(halo[1])
    leaf_first = device * LEAVES
    def sib_one(i):
        x = lev[i]
        lhs = jnp.concatenate([split(x[:, 64:]), split(x[:, :64])], axis=0)
        o = dot_nt(lhs, ls[pl.ds(2 * i, 2)].reshape(128, 64))
        sib[i] = jnp.where(first_half, o[0:16] + o[16:32], o[32:48] + o[48:64])

    ls_c.wait()

    def near_part(k):
        pltpu.make_async_copy(
            nb_h.at[pl.ds(k * per, per)], nb.at[pl.ds(k * per, per)], nb_sem.at[k]).wait()
        pltpu.make_async_copy(
            lc_h.at[pl.ds(k * lper, lper)], lc.at[pl.ds(k * lper, lper)], lc_sem.at[k]).wait()

        def near_step(g, carry):
            for u in range(12):
                s = k * per + g * 24 + 2 * u
                one, two = (
                    eh[jnp.clip(nsrc[s + i] - leaf_first + 1, 0, LEAVES + 1)] for i in range(2))
                lhs = jnp.concatenate(
                    [jnp.concatenate([one, zero], axis=1), jnp.concatenate([zero, two], axis=1)],
                    axis=0)
                o = dot_nt(lhs, jnp.concatenate([nb[s], nb[s + 1]], axis=1))
                prod[pl.ds(s, RHS, stride=SLOT_ROWS), :] = joined(o[:32])
                prod[pl.ds(s + 1, RHS, stride=SLOT_ROWS), :] = joined(o[32:])
                if u < 4:
                    sib_one(lax.rem((2 * k + g) * 4 + u, PAIRS - 1))
                if u < 8:
                    t = k * lper + g * 8 + u
                    cp[t] = jnp.concatenate([lc[t, 0], lc[t, 1], lc[t, 2], lc[t, 3]], axis=1)
            return carry

        lax.fori_loop(0, per // 24, near_step, 0)

    near_part(0)

    for i in range(1, COLS):
        peer = lax.rem(col + COLS - i, COLS)
        pltpu.make_async_remote_copy(
            xr.at[peer], xr.at[peer], xr_s.at[i], xr_r.at[i],
            device_id=(row, peer), device_id_type=MESH).wait_recv()
    for i in range(4):
        upair[i] = xr[2 * i] + xr[2 * i + 1]

    def up_upper(source, count, target, first):
        for i in range(count // 2):
            upair[target + i] = lift_two(
                upair[source + 2 * i], upair[source + 2 * i + 1],
                eu[first + 4 * i : first + 4 * i + 4])

    up_upper(0, 4, 4, 0)
    up_upper(4, 2, 6, 8)
    row_root = lift(upair[6], eu[12:14])
    zr[row] = placed(row_root, lax.rem(row, 2))
    zr_copies = []
    for i in range(1, ROWS):
        c = pltpu.make_async_remote_copy(
            zr.at[row], zr.at[row], zr_s.at[i], zr_r.at[i],
            device_id=(lax.rem(row + i, ROWS), col), device_id_type=MESH)
        c.start()
        zr_copies.append(c)

    near_part(1)
    near_part(2)
    relay_first()
    near_part(3)

    target = nt_v[...] - leaf_first
    slot = lax.broadcasted_iota(jnp.int32, (LEAVES, SLOTS), 1)
    one_hot = (
        (jnp.broadcast_to(target, (LEAVES, SLOTS))
         == lax.broadcasted_iota(jnp.int32, (LEAVES, SLOTS), 0))
        & (slot < ncnt[0])
    ).astype(BF16)

    relay_second()

    def dup_pair(owner, p):
        x = gath[owner, p]
        turned = jnp.concatenate([x[:, 64:], x[:, :64]], axis=1)
        base = owner * LEAVES + 2 * p
        dup[base] = split(jnp.where(first_half, x, turned))
        dup[base + 1] = split(jnp.where(first_half, turned, x))

    def dup_all(owner):
        def dup_step(g, carry):
            for u in range(16):
                dup_pair(owner, g * 16 + u)
            return carry

        lax.fori_loop(0, PAIRS // 16, dup_step, 0)

    twin = 1 - core
    for k in range(CHUNKS):
        recv(sibling, k, 0)
    for first, owner in ((0, col), (4, down_col), (8, up_col), (12, sibling)):

        def sum_step(g, carry, first=first, owner=owner):
            for u in range(2):
                r = first + g * 2 + u
                x = prod[pl.ds(r * SLOT_ROWS, SLOTS), :]
                high = x.astype(BF16)
                low = (x - high.astype(F32)).astype(BF16)
                nacc[pl.ds(r, LEAVES, stride=LEAF_ROWS), :] = (
                    dot_nn(one_hot, high) + dot_nn(one_hot, low))
                for v in range(8):
                    dup_pair(owner, g * 16 + u * 8 + v)
            return carry

        lax.fori_loop(0, 2, sum_step, 0)
    for kind, owner in ((4, zprev * 2 + twin), (5, znext * 2 + twin)):
        for k in range(CHUNKS):
            recv(owner, k, kind)
        dup_all(owner)
    relay_far()
    dup_all(far_col)

    halo_next.wait_send()
    halo_prev.wait_send()
    for c in sends[:-CHUNKS] + xr_copies + zr_copies:
        c.wait_send()

    for i in range(1, ROWS):
        peer = lax.rem(row + ROWS - i, ROWS)
        pltpu.make_async_remote_copy(
            zr.at[peer], zr.at[peer], zr_s.at[i], zr_r.at[i],
            device_id=(peer, col), device_id_type=MESH).wait_recv()
    for i in range(8):
        upair[7 + i] = zr[2 * i] + zr[2 * i + 1]
    up_upper(7, 8, 15, 16)
    up_upper(15, 4, 19, 32)
    up_upper(19, 2, 21, 40)

    own = []
    for j, base in enumerate((0, 4, 6, 7, 15, 19, 21)):
        own.append((base, col // (1 << j)) if j < 3 else (base, row // (1 << (j - 3))))
    y = jnp.zeros((RHS, RANK), F32)
    for j in range(6, -1, -1):
        base, mine = own[j]
        pair = upair[base + mine // 2]
        turned = jnp.concatenate([pair[:, 64:], pair[:, :64]], axis=1)
        other = jnp.where(lax.rem(mine, 2) == 1, pair, turned)[:, :64]
        y = joined(dot_nt(split(other), su[j])) + joined(dot_nt(split(y), eu[48 + j]))

    ylev[30] = placed(y, 0)
    for h in range(HEIGHT - 1, -1, -1):
        count = PAIRS >> h
        off = level_offset(h)

        def down_one(parent, p, h=h, off=off):
            w = mb[pl.ds(off + 2 * p, 2)].reshape(128, 64)
            value = joined(dot_nt(split(parent), w))
            if h:
                ylev[lev_base(h) + p] = value + sib[lev_base(h) + p]
            else:
                carried[p] = value

        if h == HEIGHT - 1:
            down_one(y, 0)
            continue

        def down_two(q, h=h, down_one=down_one):
            pair = ylev[lev_base(h + 1) + q]
            down_one(pair[:, :64], 2 * q)
            down_one(pair[:, 64:], 2 * q + 1)

        half = count // 2
        group = min(half, 8)

        def down_step(g, carry, down_two=down_two, group=group):
            for u in range(group):
                down_two(g * group + u)
            return carry

        lax.fori_loop(0, half // group, down_step, 0)

    for k in range(CHUNKS):
        recv(zfar * 2 + twin, k, 6)
    dup_all(zfar * 2 + twin)

    bt_c.wait()
    group_first = row * (LEAVES * COLS)

    def final_step(g, carry):
        pairs = [g * (FINAL // 2) + u for u in range(FINAL // 2)]

        def listed_of(t):
            d = [dup[jnp.clip(lsrc[j, t] - group_first, 0, LEAVES * COLS - 1)]
                 for j in range(PARTNERS)]
            return jnp.concatenate(
                [jnp.where(first_half2, d[0], d[1]), jnp.where(first_half2, d[2], d[3])], axis=1)

        lhs = [jnp.concatenate([listed_of(2 * q), listed_of(2 * q + 1)], axis=0) for q in pairs]
        listed = [dot_nt(x, cp[pl.ds(2 * q, 2)].reshape(128, 256)) for x, q in zip(lhs, pairs)]
        y0 = []
        for o, q in zip(listed, pairs):
            c = carried[q]
            one = jnp.where(first_half, joined(o[:32]) + c, 0.0)
            two = jnp.where(first_half, 0.0, joined(o[32:]) + c)
            y0.append(jnp.concatenate([split(one), split(two)], axis=0))
        starts = [pl.multiple_of(q * 2 * LEAF, 2 * LEAF) for q in pairs]
        far = []
        for y, start in zip(y0, starts):
            w = bt[:, pl.ds(start, 2 * LEAF)]
            far.append(dot_nn(y, jnp.concatenate([w[:, :LEAF], w[:, LEAF:]], axis=0)))
        for o, q, start in zip(far, pairs, starts):
            out[:, pl.ds(start, 2 * LEAF)] = jnp.concatenate(
                [joined(o[:32]) + nacc[pl.ds(2 * q * LEAF_ROWS, RHS), :],
                 joined(o[32:]) + nacc[pl.ds((2 * q + 1) * LEAF_ROWS, RHS), :]], axis=1)
        return carry

    lax.fori_loop(0, LEAVES // FINAL, final_step, 0)
    for c in sends[-CHUNKS:]:
        c.wait_send()


def shards(
    emission, basis_source, basis_target, local_transfer, local_sibling, upper_transfer,
    upper_sibling, leaf_source, leaf_coupling, near_block, near_target, near_source, near_count,
):
    hbm = pl.BlockSpec(memory_space=pl.ANY)
    smem = pl.BlockSpec(memory_space=pltpu.SMEM)
    vmem = pl.BlockSpec(memory_space=pltpu.VMEM)
    dma = pltpu.SemaphoreType.DMA
    V = pltpu.VMEM
    return pl.pallas_call(
        kernel,
        out_shape=V((RHS, LEAVES * LEAF), F32),
        in_specs=[hbm] * 7 + [smem, hbm, hbm, vmem, smem, smem],
        out_specs=vmem,
        scratch_shapes=[
            V((RHS, 8192), F32), V((RANK, 8192), BF16), V((RANK, 8192), BF16),
            V((64, 64, 126), BF16), V((62, 64, 64), BF16),
            V((64, 64, 254), BF16), V((64, 64, 254), BF16),
            V((LEAVES, PARTNERS, 64, 64), BF16), V((SLOTS, 128, 128), BF16),
            V((LEAVES + 2, 32, 128), BF16),
            V((2, RHS, 128), F32),
            V((COLS, PAIRS, RHS, 128), F32),
            V((COLS * LEAVES, 32, 128), BF16),
            V((128 * MAT, 128), F32),
            V((126, 64, 64), BF16),
            V((64 * MAT, 128), F32),
            V((64, 64, 64), BF16),
            V((8, 64, 64), BF16),
            V((32, RHS, 128), F32),
            V((32, RHS, 128), F32),
            V((32, RHS, 128), F32),
            V((PAIRS, RHS, 128), F32),
            V((COLS, RHS, 128), F32),
            V((ROWS, RHS, 128), F32),
            V((22, RHS, 128), F32),
            V((RHS * SLOT_ROWS, 128), F32),
            V((LEAVES * LEAF_ROWS, 128), F32),
            V((LEAVES, 64, 256), BF16),
            dma((6,)), dma((NEAR_PARTS,)), dma((NEAR_PARTS,)), dma((CHUNKS,)), dma((2,)), dma((2,)),
            dma((3, CHUNKS)), dma((4, CHUNKS)), dma((7, CHUNKS)),
            dma((COLS,)), dma((COLS,)), dma((ROWS,)), dma((ROWS,)),
        ],
        compiler_params=pltpu.CompilerParams(
            collective_id=0, has_side_effects=True, vmem_limit_bytes=58 * 1024 * 1024),
        name="h2_product",
    )(
        emission, basis_source, basis_target, local_transfer.transpose(1, 2, 0), local_sibling,
        upper_transfer.transpose(1, 2, 0), upper_sibling.transpose(1, 2, 0), leaf_source.T,
        leaf_coupling, near_block, near_target.reshape(1, SLOTS), near_source, near_count,
    )


def solution(mesh):
    both = ("row", "col")
    in_specs = (
        P(None, both), P(None, both), P(None, both), P(both, None, None), P(both, None, None),
        P(), P(), P(both, None), P(both, None, None, None), P(both, None, None),
        P(both), P(both), P(both),
    )
    return jax.shard_map(
        shards, mesh=mesh, in_specs=in_specs, out_specs=P(None, both), check_vma=False)
```
